256 devices in a mesh: ctx: 32 (over x, y, core), sub: 8 (over z).
Axes of the slice: x: 4, y: 4, z: 8, core: 2. Of those that a mesh axis runs over, the one named last changes fastest.
Arguments:
- latent_cache: bfloat16 [8, 262144, 512], P(None, ('ctx', 'sub')), may hold values from -6 to 6
- rope_cache: bfloat16 [8, 64, 262144], P(None, None, ('ctx', 'sub')), may hold values from -5 to 5
- q_latent: bfloat16 [8, 2, 128, 512], P(None, None, 'sub'), may hold values from -12 to 12
- q_rope: bfloat16 [8, 2, 8192], P(None, None, 'sub'), may hold values from -12 to 12
- lengths: int32 [8], replicated, may hold values from 16384 to 262144, as said below
Outputs:
- context: bfloat16 [2048, 512], P(('ctx', 'sub'))
The draws below stay inside these ranges and needn't reach their ends.
Inputs may be any that keep to these rules, and one draw needn't show every extreme that they name: `lengths`: the longest sequence has exactly 262144 cached positions.
All inputs are finite; a program needn't handle non-finite values.
Results may differ from the reference program's by a relative error of at most 0.0045.
Values may be sent and summed in bfloat16 or wider, within the bound.
A program may use at most 64 MiB of HBM per device.

```python
import jax
import jax.numpy as jnp
from jax import lax

HEADS = 128
LAT = 512
ROPE = 64
NOPE = 128
QTOK = 2
BATCH = 8
LMAX = 262144


def first_positions(key):
    shared = jax.random.fold_in(key, 101)
    return jax.random.randint(shared, (BATCH,), 0, LMAX // 16 - 2)


def anchor_rows(key):
    shared = jax.random.fold_in(key, 103)
    magnitude = jax.random.uniform(shared, (BATCH, LAT), jnp.float32, 3.5, 5.0)
    signs = jax.random.bernoulli(jax.random.fold_in(shared, 7), 0.5, (BATCH, LAT))
    return jnp.where(signs, magnitude, -magnitude)


def plant_pair(values, anchor, start):
    paired = anchor.reshape(LAT // 2, 2)
    rotated = jnp.stack([paired[:, 1], -paired[:, 0]], axis=1).reshape(LAT)
    second = 0.99 * anchor + 0.2 * rotated
    values = values.at[start].set(anchor)
    return values.at[start + 1].set(second)


def draw_latent_cache(key, part):
    shared = key
    key = jax.random.fold_in(key, 1)
    anchors = anchor_rows(shared)
    firsts = first_positions(shared)

    def per_sequence(seq_index):
        seq_key = jax.random.fold_in(key, seq_index)
        values = jnp.clip(jax.random.normal(seq_key, (LMAX, LAT), jnp.float32), -5.0, 5.0)
        values = plant_pair(values, anchors[seq_index], firsts[seq_index])
        return values.astype(jnp.bfloat16)
    return lax.map(per_sequence, jnp.arange(BATCH, dtype=jnp.int32))


def plant_queries(values, anchors):
    score_scale = (NOPE + ROPE) ** (-0.5)
    head_ids = jnp.arange(HEADS, dtype=jnp.int32)
    group = (head_ids // 16).astype(jnp.float32)
    target = 100.0 + 120.0 * group / max(HEADS // 16 - 1, 1)
    squared = jnp.sum(anchors * anchors, axis=1)
    strength = target[None, :] / (squared[:, None] * score_scale)
    token_ids = jnp.arange(QTOK, dtype=jnp.int32)
    aligned = (head_ids % 16 == 0)[None, None, :, None] & (token_ids == 0)[None, :, None, None]
    planted = strength[:, None, :, None] * anchors[:, None, None, :]
    return jnp.where(aligned, planted, values)


def draw_q_latent(key, part):
    shared = key
    key = jax.random.fold_in(key, 2)
    anchors = anchor_rows(shared)
    values = jnp.clip(2.5 * jax.random.normal(key, (BATCH, QTOK, HEADS, LAT), jnp.float32), -12.0, 12.0)
    return plant_queries(values, anchors).astype(jnp.bfloat16)


def draw_q_rope(key, part):
    key = jax.random.fold_in(key, 3)
    values = jnp.clip(2.5 * jax.random.normal(key, (BATCH, QTOK, HEADS * ROPE), jnp.float32), -12.0, 12.0)
    column_head = jnp.arange(HEADS * ROPE, dtype=jnp.int32) // ROPE
    token_ids = jnp.arange(QTOK, dtype=jnp.int32)
    aligned = (column_head % 16 == 0)[None, None, :] & (token_ids == 0)[None, :, None]
    values = jnp.where(aligned, 0.0, values)
    return values.astype(jnp.bfloat16)


def draw_lengths(key, part):
    key = jax.random.fold_in(key, 4)
    drawn = jax.random.randint(jax.random.fold_in(key, 1), (BATCH,), LMAX // 16, LMAX + 1)
    longest = jax.random.randint(jax.random.fold_in(key, 2), (), 0, BATCH)
    return jnp.where(jnp.arange(BATCH, dtype=jnp.int32) == longest, LMAX, drawn).astype(jnp.int32)


def block_levels(stream_key, extent, split, smallest, largest):
    loudness = 1.0
    for axis_at, parts in split:
        steps = jax.random.uniform(jax.random.fold_in(jax.random.fold_in(stream_key, 6), axis_at), (parts,), jnp.float32, smallest / len(split), largest / len(split))
        loudness = loudness * jnp.repeat(jnp.exp(steps), extent[axis_at] // parts).reshape((-1,) + (1,) * (len(extent) - 1 - axis_at))
    return loudness


def noise(key, shape, deviation, limit, split=(), held_as=jnp.bfloat16):
    values = jax.random.normal(key, shape, jnp.float32) * deviation
    if len(split) > 0:
        values = block_levels(key, shape, split, -0.22, 0.18) * values
    return jnp.clip(values, min=-limit, max=limit).astype(held_as)


def setup_inputs(seed: int = 0) -> dict:
    streams_of = jax.random.split(jax.random.key(seed), 6)
    latent_cache = draw_latent_cache(jax.random.fold_in(streams_of[5], 71), 0)
    rope_cache = noise(streams_of[1], (BATCH, ROPE, LMAX), 1.0, 5.0, ((2, 256),))
    q_latent = draw_q_latent(jax.random.fold_in(streams_of[5], 71), 0)
    q_rope = draw_q_rope(jax.random.fold_in(streams_of[5], 71), 0)
    lengths = draw_lengths(jax.random.fold_in(streams_of[5], 71), 0)
    return dict(latent_cache=latent_cache, rope_cache=rope_cache, q_latent=q_latent, q_rope=q_rope, lengths=lengths)


def reference(latent_cache, rope_cache, q_latent, q_rope, lengths):
    score_scale = (NOPE + ROPE) ** -0.5
    row_count = QTOK * HEADS
    positions = jnp.arange(LMAX, dtype=jnp.int32)
    offsets = jnp.repeat(jnp.arange(QTOK, dtype=jnp.int32) - (QTOK - 1), HEADS)

    def per_sequence(pieces):
        latent_rows, rope_rows, query_lat, query_rope, seq_length = pieces
        query_lat = query_lat.reshape(row_count, LAT)
        query_rope = query_rope.reshape(row_count, ROPE)
        scores = jnp.dot(query_lat, latent_rows.T, preferred_element_type=jnp.float32)
        scores = scores + jnp.dot(query_rope, rope_rows, preferred_element_type=jnp.float32)
        scores = scores * score_scale
        visible_end = seq_length + offsets
        visible = positions[None, :] < visible_end[:, None]
        row_top = jnp.max(jnp.where(visible, scores, -1e30), axis=1)
        weights = jnp.where(visible, jnp.exp(scores - row_top[:, None]), 0.0)
        row_total = jnp.sum(weights, axis=1)
        numerator = jnp.dot(weights.astype(jnp.bfloat16), latent_rows, preferred_element_type=jnp.float32)
        return (numerator / row_total[:, None]).astype(jnp.bfloat16)

    context = lax.map(per_sequence, (latent_cache, rope_cache, q_latent, q_rope, lengths))
    return context.reshape(BATCH * row_count, LAT)
```

```python
import functools

import jax
import jax.numpy as jnp
from jax import lax
from jax.experimental import pallas as pl
from jax.experimental.pallas import tpu as pltpu
from jax.sharding import PartitionSpec as P

MESH = pl.DeviceIdType.MESH
NOPE = 128
QTOK = 2
NX, NY, NC, NZ = 4, 4, 2, 8
LOG2E = 1.4426950408889634
FLOOR = -16384.0


def place():
    ctx = lax.axis_index("ctx")
    return ctx // (NY * NC), (ctx // NC) % NY, ctx % NC, lax.axis_index("sub")


def device(x, y, c, z):
    return ((x * NY + y) * NC + c, z)


def split3(v):
    hi = v.astype(jnp.bfloat16).astype(jnp.float32)
    rest = v - hi
    mid = rest.astype(jnp.bfloat16).astype(jnp.float32)
    return hi, mid, rest - mid


def lanes(shape):
    return lax.broadcasted_iota(jnp.int32, shape, len(shape) - 1)


def pack_rows(num, top, total):
    rows = num.shape[0]
    t1, t2, t3 = split3(top)
    l1, l2, _ = split3(total)
    lane = lanes((rows, 128))
    stats = jnp.where(
        lane < 16, t1, jnp.where(lane < 32, t2, jnp.where(lane < 48, t3, jnp.where(lane < 64, l1, l2)))
    )
    return jnp.concatenate([num.astype(jnp.bfloat16), stats.astype(jnp.bfloat16)], axis=1)


def unpack_rows(message):
    num = message[:, :512].astype(jnp.float32)
    stats = message[:, 512:].astype(jnp.float32)
    top = stats[:, 0:1] + stats[:, 16:17] + stats[:, 32:33]
    total = stats[:, 48:49] + stats[:, 64:65]
    return num, top, total


def merge(parts):
    top = functools.reduce(jnp.maximum, [p[1] for p in parts])
    factors = [jnp.exp2(p[1] - top) for p in parts]
    num = functools.reduce(jnp.add, [p[0] * f for p, f in zip(parts, factors)])
    total = functools.reduce(jnp.add, [p[2] * f for p, f in zip(parts, factors)])
    return num, top, total


def pack_owner(num, top, total):
    t1, t2, t3 = split3(top)
    l1, l2, _ = split3(total)
    lane = lanes((64, 128))
    tops = jnp.where(lane < 16, t1, jnp.where(lane < 32, t2, t3)).reshape(8, 8, 128)
    totals = jnp.where(lane < 16, l1, l2).reshape(8, 8, 128)
    num = num.reshape(8, 8, 512)
    left = jnp.concatenate([num[:, :, :256], tops], axis=2)
    right = jnp.concatenate([num[:, :, 256:], totals], axis=2)
    return jnp.concatenate([left, right], axis=1).astype(jnp.bfloat16)


def kernel(
    lat_hbm, rope_hbm, q_hbm, qr_hbm, lengths, out,
    kv, rr, q, qr, num, core_in, x_out, x_in, y_out, y_in, z_out, z_in,
    kv_sem, own_sem, zq_send, zq_recv, rz_send, rz_recv, yq_send, yq_recv, rx_send, rx_recv,
    cq_send, cq_recv, cr_send, cr_recv, ce_send, ce_recv, x_send, x_recv, y_send, y_recv, z_send, z_recv,
):
    x, y, c, z = place()
    positions = kv.shape[1]
    first = ((x * NY + y) * NC + c) * NZ * positions + z * positions
    scale = (NOPE + 64) ** -0.5 * LOG2E
    my_j = y // 2

    def wrap_x(d):
        return (x + d) % NX

    def wrap_y(d):
        return (y + d) % NY

    def wrap_z(d):
        return (z + d) % NZ

    def step_dx(k):
        return jnp.where(k < 2, 2, jnp.where(k >= 6, 0, jnp.where(k % 2 == 0, 1, 3)))

    def step_j(k):
        early = jnp.where(k < 2, k, jnp.where(k < 4, 0, 1))
        return jnp.where(k < 6, early, jnp.where(k == 6, 1 - my_j, my_j))

    def step_seq(k):
        return wrap_x(step_dx(k)) * 2 + step_j(k)

    def load_kv(k):
        b = step_seq(k)
        return (
            pltpu.make_async_copy(lat_hbm.at[b], kv.at[k], kv_sem.at[k, 0]),
            pltpu.make_async_copy(rope_hbm.at[b], rr.at[k, pl.ds(0, 64)], kv_sem.at[k, 1]),
            pltpu.make_async_copy(rope_hbm.at[b], rr.at[k, pl.ds(64, 64)], kv_sem.at[k, 2]),
        )

    def remote(src, dst, send, recv, target):
        return pltpu.make_async_remote_copy(
            src_ref=src, dst_ref=dst, send_sem=send, recv_sem=recv, device_id=target, device_id_type=MESH
        )

    tile = pl.ds(pl.multiple_of(y * 128, 128), 128)

    own_q = pltpu.make_async_copy(q_hbm.at[:, c, :, tile], q.at[:, z, c, :, tile], own_sem.at[0])
    own_r = pltpu.make_async_copy(qr_hbm.at[2 * x + c], qr.at[c, x, z], own_sem.at[1])

    def zq(b, d):
        return remote(
            q_hbm.at[b, c, :, tile], q.at[b, z, c, :, tile], zq_send.at[b, d - 1], zq_recv.at[b, d - 1],
            device(x, y, c, wrap_z(d)),
        )

    def rz(d):
        return remote(
            qr_hbm.at[2 * x + c], qr.at[c, x, z], rz_send.at[d - 1], rz_recv.at[d - 1], device(x, y, c, wrap_z(d))
        )

    def yq(b, d):
        return remote(
            q.at[b, :, c, :, tile], q.at[b, :, c, :, tile], yq_send.at[b, d - 1], yq_recv.at[b, d - 1],
            device(x, wrap_y(d), c, z),
        )

    def rx(d):
        return remote(qr.at[c, x], qr.at[c, x], rx_send.at[d - 1], rx_recv.at[d - 1], device(wrap_x(d), y, c, z))

    def cq(b):
        return remote(q.at[b, :, c], q.at[b, :, c], cq_send.at[b], cq_recv.at[b], device(x, y, 1 - c, z))

    def cr():
        return remote(qr.at[c], qr.at[c], cr_send, cr_recv, device(x, y, 1 - c, z))

    def ce(k):
        return remote(num.at[k, 1 - c], core_in.at[k], ce_send.at[k], ce_recv.at[k], device(x, y, 1 - c, z))

    def xs(k):
        d = step_dx(k)
        j = step_j(k)
        return remote(
            x_out.at[k], x_in.at[d - 1, j], x_send.at[k], x_recv.at[d - 1, j], device(wrap_x(d), y, c, z)
        )

    def xr(d, j):
        return remote(
            x_out.at[0], x_in.at[d - 1, j], x_send.at[0], x_recv.at[d - 1, j], device(wrap_x(d), y, c, z)
        )

    def ys(t):
        return remote(
            y_out.at[t], y_in.at[y % 2], y_send.at[t], y_recv.at[y % 2], device(x, (1 - my_j) * 2 + t, c, z)
        )

    def yr(s):
        return remote(
            y_out.at[s], y_in.at[s], y_send.at[s], y_recv.at[s], device(x, (1 - my_j) * 2 + s, c, z)
        )

    y_pair = my_j * 2 + (1 - y % 2)

    def zs(column, d):
        return remote(
            z_out.at[column, wrap_z(d)], z_in.at[column, z], z_send.at[column, d], z_recv.at[column, d],
            device(x, jnp.where(column == 0, y, y_pair), c, wrap_z(d)),
        )

    def zr(column, d):
        source = (z - d + NZ) % NZ
        return remote(
            z_out.at[column, z], z_in.at[column, source], z_send.at[column, d], z_recv.at[column, d],
            device(x, y_pair, c, wrap_z(d)),
        )

    for k in range(2):
        for copy in load_kv(k):
            copy.start()
    own_q.start()
    own_r.start()
    partners = [device(x, y, 1 - c, z)]
    partners += [device(wrap_x(d), y, c, z) for d in (1, 2, 3)]
    partners += [device(x, (1 - my_j) * 2 + t, c, z) for t in (0, 1)]
    partners += [device(x, y, c, wrap_z(d)) for d in range(1, NZ)]
    partners += [device(x, y_pair, c, wrap_z(d)) for d in range(NZ)]
    barrier = pltpu.get_barrier_semaphore()
    for partner in partners:
        pl.semaphore_signal(barrier, inc=1, device_id=partner, device_id_type=MESH)

    def load_rest(k, carry):
        for copy in load_kv(k):
            copy.start()
        return carry

    lax.fori_loop(2, 8, load_rest, 0)
    pl.semaphore_wait(barrier, len(partners))

    z_order = (4, 3, 5, 2, 6, 1, 7)
    for d in z_order:
        rz(d).start()

    def send_z(k, carry):
        b = step_seq(k)
        for d in z_order:
            zq(b, d).start()
        return carry

    lax.fori_loop(0, 8, send_z, 0)
    own_r.wait()
    own_q.wait()

    for d in z_order:
        rz(d).wait_recv()
    for d in (2, 1, 3):
        rx(d).start()

    def send_y(k, carry):
        b = step_seq(k)
        for d in z_order:
            zq(b, d).wait_recv()
        for d in (2, 1, 3):
            yq(b, d).start()
        return carry

    lax.fori_loop(0, 8, send_y, 0)
    for d in (1, 2, 3):
        rx(d).wait_recv()
    cr().start()

    def send_core(k):
        b = step_seq(k)
        for d in (1, 2, 3):
            yq(b, d).wait_recv()
        cq(b).start()

    send_core(0)
    cr().wait_recv()

    rows_q = (NZ, QTOK, 16)

    def compute(k):
        b = step_seq(k)
        cq(b).wait_recv()
        for copy in load_kv(k):
            copy.wait()
        query = q[b].reshape(256, 512)
        rope_q = qr[b % 2, b // 2]
        half = lanes((NZ, 16, 128)) // 64
        zero = jnp.zeros_like(rope_q)
        rope_q = jnp.stack([jnp.where(half == t, rope_q, zero) for t in range(QTOK)], axis=1).reshape(256, 128)
        latent = kv[k]
        scores = lax.dot_general(query, latent, (((1,), (1,)), ((), ())), preferred_element_type=jnp.float32)
        scores = scores + jnp.dot(rope_q, rr[k], preferred_element_type=jnp.float32)
        position = first + lanes((1, positions))
        bias = jnp.concatenate(
            [jnp.where(position < lengths[b] - (QTOK - 1 - t), 0.0, -1e30) for t in range(QTOK)], axis=0
        )
        scores = scores.reshape(*rows_q, positions) * scale + bias.reshape(1, QTOK, 1, positions)
        scores = scores.reshape(256, positions)
        top = jnp.maximum(jnp.max(scores, axis=1, keepdims=True), FLOOR)
        weights = jnp.exp2(scores - top)
        total = jnp.sum(weights, axis=1, keepdims=True)
        part = jnp.dot(weights.astype(jnp.bfloat16), latent, preferred_element_type=jnp.float32)
        stats = jnp.where(lanes((256, 128)) < 64, top, total)
        num[k, :, :, 0:512] = part.reshape(2, 128, 512)
        num[k, :, :, 512:640] = stats.reshape(2, 128, 128)
        ce(k).start()

    def core_merged(k):
        ce(k).wait_recv()
        mine = num[k, c]
        other = core_in[k]
        return merge([(a[:, :512], a[:, 512:513], a[:, 576:577]) for a in (mine, other)])

    def step(k, carry):
        send_core(k + 1)
        compute(k)

        @pl.when(k >= 1)
        def _():
            x_out[k - 1] = pack_rows(*core_merged(k - 1))
            xs(k - 1).start()

        return carry

    lax.fori_loop(0, 7, step, 0)
    compute(7)

    def own_pair(k, j):
        parts = [core_merged(k)]
        for d in (2, 1, 3):
            xr(d, j).wait_recv()
            parts.append(unpack_rows(x_in[d - 1, j]))
        return merge(parts)

    def token(a, t):
        return a.reshape(4, QTOK, 16, a.shape[1])[:, t].reshape(64, a.shape[1])

    merged = own_pair(6, 1 - my_j)
    for t in range(QTOK):
        y_out[t] = pack_rows(*[token(a, t) for a in merged])
        ys(t).start()

    merged = own_pair(7, my_j)
    mine = y % 2
    tokens = [[token(a, t) for a in merged] for t in range(QTOK)]
    other = [jnp.where(mine == 0, b, a) for a, b in zip(*tokens)]
    z_out[1] = pack_owner(*other)
    for d in (4, 3, 5, 2, 6, 1, 7, 0):
        zs(1, d).start()
    parts = [tuple(jnp.where(mine == 0, a, b) for a, b in zip(*tokens))]
    for s in range(2):
        yr(s).wait_recv()
        parts.append(unpack_rows(y_in[s]))
    z_out[0] = pack_owner(*merge(parts))
    for d in z_order:
        zs(0, d).start()
    z_in[0, z] = z_out[0, z]
    for d in range(1, NZ):
        zr(0, d).wait_recv()
    for d in range(NZ):
        zr(1, d).wait_recv()

    got = z_in[...].reshape(16, 16, 384).astype(jnp.float32)
    tops = got[:, :8, 256:]
    totals = got[:, 8:, 256:]
    tops = tops[:, :, 0:1] + tops[:, :, 16:17] + tops[:, :, 32:33]
    totals = totals[:, :, 0:1] + totals[:, :, 16:17]
    top = jnp.max(tops, axis=0, keepdims=True)
    factor = jnp.exp2(tops - top)
    total = jnp.sum(totals * factor, axis=0)
    left = jnp.sum(got[:, :8, :256] * factor, axis=0)
    right = jnp.sum(got[:, 8:, :256] * factor, axis=0)
    out[...] = (jnp.concatenate([left, right], axis=1) / total).astype(jnp.bfloat16)

    for d in range(1, NZ):
        rz(d).wait_send()
        zs(0, d).wait_send()
    for d in range(NZ):
        zs(1, d).wait_send()
    for d in (1, 2, 3):
        rx(d).wait_send()
    cr().wait_send()
    for t in range(QTOK):
        ys(t).wait_send()

    def drain(k, carry):
        for d in range(1, NZ):
            zq(k, d).wait_send()
        for d in (1, 2, 3):
            yq(k, d).wait_send()
        cq(k).wait_send()
        ce(k).wait_send()
        return carry

    lax.fori_loop(0, 8, drain, 0)

    def drain_x(k, carry):
        xs(k).wait_send()
        return carry

    lax.fori_loop(0, 6, drain_x, 0)


def body(latent_cache, rope_cache, q_latent, q_rope, lengths):
    batch, positions, width = latent_cache.shape
    heads = q_latent.shape[2]
    rope_q = q_rope.reshape(batch, QTOK, heads, 64).transpose(0, 2, 1, 3).reshape(batch, heads, 128)
    anywhere = pl.BlockSpec(memory_space=pl.ANY)
    dma = pltpu.SemaphoreType.DMA
    return pl.pallas_call(
        kernel,
        out_shape=jax.ShapeDtypeStruct((8, width), jnp.bfloat16),
        in_specs=[anywhere] * 4 + [pl.BlockSpec(memory_space=pltpu.SMEM)],
        out_specs=pl.BlockSpec(memory_space=pltpu.VMEM),
        scratch_shapes=[
            pltpu.VMEM((8, positions, width), jnp.bfloat16),
            pltpu.VMEM((8, 128, positions), jnp.bfloat16),
            pltpu.VMEM((8, NZ, QTOK, 16, width), jnp.bfloat16),
            pltpu.VMEM((2, 4, NZ, 16, 128), jnp.bfloat16),
            pltpu.VMEM((8, 2, 128, 640), jnp.float32),
            pltpu.VMEM((8, 128, 640), jnp.float32),
            pltpu.VMEM((6, 128, 640), jnp.bfloat16),
            pltpu.VMEM((3, 2, 128, 640), jnp.bfloat16),
            pltpu.VMEM((2, 64, 640), jnp.bfloat16),
            pltpu.VMEM((2, 64, 640), jnp.bfloat16),
            pltpu.VMEM((2, 8, 16, 384), jnp.bfloat16),
            pltpu.VMEM((2, 8, 16, 384), jnp.bfloat16),
            dma((8, 3)), dma((2,)),
            dma((8, 7)), dma((8, 7)), dma((7,)), dma((7,)),
            dma((8, 3)), dma((8, 3)), dma((3,)), dma((3,)),
            dma((8,)), dma((8,)), dma, dma,
            dma((8,)), dma((8,)),
            dma((6,)), dma((3, 2)), dma((2,)), dma((2,)),
            dma((2, 8)), dma((2, 8)),
        ],
        compiler_params=pltpu.CompilerParams(
            collective_id=0, has_side_effects=True, vmem_limit_bytes=56 * 2**20
        ),
        cost_estimate=pl.CostEstimate(flops=5 * 10**9, bytes_accessed=10 * 10**6, transcendentals=2 * 10**6),
    )(latent_cache, rope_cache, q_latent, rope_q, lengths)


def solution(mesh):
    in_specs = (
        P(None, ("ctx", "sub"), None),
        P(None, None, ("ctx", "sub")),
        P(None, None, "sub", None),
        P(None, None, "sub"),
        P(),
    )
    out_specs = P(("ctx", "sub"), None)
    return jax.shard_map(body, mesh=mesh, in_specs=in_specs, out_specs=out_specs, check_vma=False)
```

```python
import functools

import jax
import jax.numpy as jnp
from jax import lax
from jax.experimental import pallas as pl
from jax.experimental.pallas import tpu as pltpu
from jax.sharding import PartitionSpec as P

MESH = pl.DeviceIdType.MESH
NOPE = 128
QTOK = 2
NX, NY, NC, NZ = 4, 4, 2, 8
LOG2E = 1.4426950408889634
FLOOR = -16384.0


def place():
    ctx = lax.axis_index("ctx")
    return ctx // (NY * NC), (ctx // NC) % NY, ctx % NC, lax.axis_index("sub")


def device(x, y, c, z):
    return ((x * NY + y) * NC + c, z)


def iota(shape, axis):
    return lax.broadcasted_iota(jnp.int32, shape, axis)


def lanes(shape):
    return iota(shape, len(shape) - 1)


def to_row(column, offset=0):
    shape = (column.shape[0], 128)
    return jnp.sum(jnp.where(lanes(shape) == iota(shape, 0) + offset, column, 0.0), axis=0, keepdims=True)


def to_column(row, rows, offset=0):
    shape = (rows, 128)
    return jnp.sum(jnp.where(lanes(shape) == iota(shape, 0) + offset, row, 0.0), axis=1, keepdims=True)


def merge(parts):
    top = functools.reduce(jnp.maximum, [p[1] for p in parts])
    factors = [jnp.exp2(p[1] - top) for p in parts]
    num = functools.reduce(jnp.add, [p[0] * f for p, f in zip(parts, factors)])
    total = functools.reduce(jnp.add, [p[2] * f for p, f in zip(parts, factors)])
    return num, top, total


class Pair:
    def __init__(self, *copies):
        self.copies = copies

    def start(self):
        for copy in self.copies:
            copy.start()

    def wait_send(self):
        for copy in self.copies:
            copy.wait_send()

    def wait_recv(self):
        for copy in self.copies:
            copy.wait_recv()


def kernel(
    lat_hbm, rope_hbm, q_hbm, qr_hbm, lengths, out,
    kv, rr, q, qr_in, qr, num, core_in,
    x_out, x_ost, x_in, x_ist, y_out, y_ost, y_in, y_ist, v_out, v_ost, v_in, v_ist,
    w_out, w_ost, w_in, w_ist, z_out, z_ost, z_in, z_ist,
    kv_sem, own_sem, zq_send, zq_recv, rz_send, rz_recv, pq_send, pq_recv, rx_send, rx_recv,
    cq_send, cq_recv, cr_send, cr_recv, ce_send, ce_recv,
    x_send, x_recv, y_send, y_recv, v_send, v_recv, w_send, w_recv, z_send, z_recv,
):
    x, y, c, z = place()
    positions = kv.shape[1]
    first = (((x * NY + y) * NC + c) * NZ + z) * positions
    scale = (NOPE + 64) ** -0.5 * LOG2E
    my_j = y // 2
    y_pair = my_j * 2 + (1 - y % 2)

    def wrap_x(d):
        return (x + d) % NX

    def wrap_y(d):
        return (y + d) % NY

    def wrap_z(d):
        return (z + d) % NZ

    def step_dx(k):
        return jnp.where(k < 2, 2, jnp.where(k >= 6, 0, jnp.where(k % 2 == 0, 1, 3)))

    def step_j(k):
        late = (k == 4) | (k == 5) | (k == 7)
        return jnp.where(k < 2, k, jnp.where(late, my_j, 1 - my_j))

    def step_pair(k):
        return wrap_x(step_dx(k))

    def load_kv(k):
        b = step_pair(k) * 2 + step_j(k)
        return (
            pltpu.make_async_copy(lat_hbm.at[b], kv.at[k], kv_sem.at[k, 0]),
            pltpu.make_async_copy(rope_hbm.at[b], rr.at[k, pl.ds(0, 64)], kv_sem.at[k, 1]),
            pltpu.make_async_copy(rope_hbm.at[b], rr.at[k, pl.ds(64, 64)], kv_sem.at[k, 2]),
        )

    def remote(src, dst, send, recv, target):
        return pltpu.make_async_remote_copy(
            src_ref=src, dst_ref=dst, send_sem=send, recv_sem=recv, device_id=target, device_id_type=MESH
        )

    def lane_tile(i):
        return pl.ds(pl.multiple_of(i * 128, 128), 128)

    tiles = (lane_tile(y), lane_tile(x))

    own_q = [
        pltpu.make_async_copy(q_hbm.at[:, j, c, :, tiles[j]], q.at[:, j, z, c, :, tiles[j]], own_sem.at[j])
        for j in range(2)
    ]
    own_r = pltpu.make_async_copy(qr_hbm.at[2 * x + c], qr_in, own_sem.at[2])

    def zq(p, j, d):
        return remote(
            q_hbm.at[p, j, c, :, tiles[j]], q.at[p, j, z, c, :, tiles[j]],
            zq_send.at[p, j, d - 1], zq_recv.at[p, j, d - 1], device(x, y, c, wrap_z(d)),
        )

    def rz(d):
        return remote(
            qr.at[c, x, z], qr.at[c, x, z], rz_send.at[d - 1], rz_recv.at[d - 1], device(x, y, c, wrap_z(d))
        )

    def pq(p, j, d):
        target = device(x, wrap_y(d), c, z) if j == 0 else device(wrap_x(d), y, c, z)
        return remote(
            q.at[p, j, :, c, :, tiles[j]], q.at[p, j, :, c, :, tiles[j]],
            pq_send.at[p, j, d - 1], pq_recv.at[p, j, d - 1], target,
        )

    def pq_wait(p, j, d):
        piece = q.at[p, j, :, c, :, pl.ds(0, 128)]
        return remote(
            piece, piece, pq_send.at[p, j, d - 1], pq_recv.at[p, j, d - 1], device(x, wrap_y(d), c, z)
        )

    def rx(d):
        return remote(qr.at[c, x], qr.at[c, x], rx_send.at[d - 1], rx_recv.at[d - 1], device(wrap_x(d), y, c, z))

    def cq(p, j):
        return remote(
            q.at[p, j, :, c], q.at[p, j, :, c], cq_send.at[p, j], cq_recv.at[p, j], device(x, y, 1 - c, z)
        )

    def cr():
        return remote(qr.at[c], qr.at[c], cr_send, cr_recv, device(x, y, 1 - c, z))

    def ce(k):
        return remote(num.at[k, 1 - c], core_in.at[k], ce_send.at[k], ce_recv.at[k], device(x, y, 1 - c, z))

    def xs(k):
        side = k % 2
        j = step_j(k)
        target = device(wrap_x(1 + 2 * side), y, c, z)
        return Pair(
            remote(x_out.at[k - 2], x_in.at[side, j], x_send.at[0, k - 2], x_recv.at[0, side, j], target),
            remote(x_ost.at[k - 2], x_ist.at[side, j], x_send.at[1, k - 2], x_recv.at[1, side, j], target),
        )

    def xr(side, j):
        target = device(wrap_x(1), y, c, z)
        return Pair(
            remote(x_out.at[0], x_in.at[side, j], x_send.at[0, 0], x_recv.at[0, side, j], target),
            remote(x_ost.at[0], x_ist.at[side, j], x_send.at[1, 0], x_recv.at[1, side, j], target),
        )

    def ys(d):
        target = device(x, wrap_y(d), c, z)
        unit = wrap_y(d)
        return Pair(
            remote(y_out.at[unit], y_in.at[d - 1], y_send.at[0, d - 1], y_recv.at[0, d - 1], target),
            remote(y_ost.at[unit], y_ist.at[d - 1], y_send.at[1, d - 1], y_recv.at[1, d - 1], target),
        )

    def vs():
        target = device(wrap_x(2), y, c, z)
        return Pair(
            remote(v_out, v_in, v_send.at[0], v_recv.at[0], target),
            remote(v_ost, v_ist, v_send.at[1], v_recv.at[1], target),
        )

    def ws(t):
        target = device(x, (1 - my_j) * 2 + t, c, z)
        slot = y % 2
        return Pair(
            remote(w_out.at[t], w_in.at[slot], w_send.at[0, t], w_recv.at[0, slot], target),
            remote(w_ost.at[t], w_ist.at[slot], w_send.at[1, t], w_recv.at[1, slot], target),
        )

    def wr(s):
        target = device(x, (1 - my_j) * 2 + s, c, z)
        return Pair(
            remote(w_out.at[s], w_in.at[s], w_send.at[0, s], w_recv.at[0, s], target),
            remote(w_ost.at[s], w_ist.at[s], w_send.at[1, s], w_recv.at[1, s], target),
        )

    def zs(column, d):
        target = device(x, y if column == 0 else y_pair, c, wrap_z(d))
        there = wrap_z(d)
        return Pair(
            remote(z_out.at[column, there], z_in.at[column, z], z_send.at[0, column, d], z_recv.at[0, column, d], target),
            remote(z_ost.at[column, there], z_ist.at[column, z], z_send.at[1, column, d], z_recv.at[1, column, d], target),
        )

    def zr(column, d):
        source = (z - d + NZ) % NZ
        target = device(x, y_pair, c, wrap_z(d))
        return Pair(
            remote(z_out.at[column, z], z_in.at[column, source], z_send.at[0, column, d], z_recv.at[0, column, d], target),
            remote(z_ost.at[column, z], z_ist.at[column, source], z_send.at[1, column, d], z_recv.at[1, column, d], target),
        )

    partners = [device(x, y, c, wrap_z(d)) for d in range(1, NZ)]
    partners += [device(wrap_x(d), y, c, z) for d in (1, 2, 3)]
    partners += [device(x, wrap_y(d), c, z) for d in (1, 2, 3)]
    partners += [device(x, y, 1 - c, z)]
    barrier = pltpu.get_barrier_semaphore()
    for partner in partners:
        pl.semaphore_signal(barrier, inc=1, device_id=partner, device_id_type=MESH)
    own_r.start()
    for copy in own_q:
        copy.start()

    def load(k, carry):
        for copy in load_kv(k):
            copy.start()
        return carry

    lax.fori_loop(0, 8, load, 0)
    own_r.wait()
    spread = (lanes((16, 1024)) // 64) == iota((16, 1024), 0)
    head = iota((16, 128), 0)
    own_rope = jnp.zeros((16, 128), jnp.float32)
    raw = qr_in[...].astype(jnp.float32)
    for t in range(QTOK):
        wide = jnp.where(spread, raw[t : t + 1], 0.0)
        narrow = functools.reduce(jnp.add, [wide[:, i * 128 : (i + 1) * 128] for i in range(8)])
        own_rope = own_rope + jnp.where(head % 2 == t, narrow, pltpu.roll(narrow, 64, 1))
    qr[c, x, z] = own_rope.astype(jnp.bfloat16)
    pl.semaphore_wait(barrier, len(partners))

    z_order = (4, 3, 5, 2, 6, 1, 7)
    pair_order = (2, 1, 3, 0)
    for d in z_order:
        rz(d).start()

    def send_z(p, j):
        for d in z_order:
            zq(p, j, d).start()

    def wait_z(p, j):
        for d in z_order:
            zq(p, j, d).wait_recv()

    send_z(wrap_x(2), 0)
    for dx in pair_order:
        send_z(wrap_x(dx), 1)
    for dx in pair_order[1:]:
        send_z(wrap_x(dx), 0)
    for copy in own_q:
        copy.wait()

    for d in z_order:
        rz(d).wait_recv()
    for d in (2, 1, 3):
        rx(d).start()
    wait_z(wrap_x(2), 0)
    for d in (2, 1, 3):
        pq(wrap_x(2), 0, d).start()
    for dx in pair_order:
        wait_z(wrap_x(dx), 1)
    for dx in pair_order:
        for d in (2, 1, 3):
            pq(wrap_x(d + dx), 1, d).start()
    for dx in pair_order[1:]:
        wait_z(wrap_x(dx), 0)
        for d in (2, 1, 3):
            pq(wrap_x(dx), 0, d).start()

    def send_core(k):
        p, j = step_pair(k), step_j(k)
        for d in (1, 2, 3):
            pq_wait(p, j, d).wait_recv()
        cq(p, j).start()

    send_core(0)
    for d in (1, 2, 3):
        rx(d).wait_recv()
    cr().start()

    def compute(k):
        p, j = step_pair(k), step_j(k)
        cq(p, j).wait_recv()
        for copy in load_kv(k):
            copy.wait()
        query = q[p, j].reshape(256, 512)
        rope_q = qr[j, p]
        half = lanes((NZ, 16, 128)) // 64
        zero = jnp.zeros_like(rope_q)
        rope_q = jnp.stack([jnp.where(half == t, rope_q, zero) for t in range(QTOK)], axis=1).reshape(256, 128)
        latent = kv[k]
        scores = lax.dot_general(query, latent, (((1,), (1,)), ((), ())), preferred_element_type=jnp.float32)
        scores = scores + jnp.dot(rope_q, rr[k], preferred_element_type=jnp.float32)
        position = first + lanes((1, positions))
        length = lengths[p * 2 + j]
        bias = jnp.concatenate(
            [jnp.where(position < length - (QTOK - 1 - t), 0.0, -1e30) for t in range(QTOK)], axis=0
        )
        scores = scores.reshape(NZ, QTOK, 16, positions) * scale + bias.reshape(1, QTOK, 1, positions)
        scores = scores.reshape(256, positions)
        top = jnp.maximum(jnp.max(scores, axis=1, keepdims=True), FLOOR)
        weights = jnp.exp2(scores - top)
        total = jnp.sum(weights, axis=1, keepdims=True)
        part = jnp.dot(weights.astype(jnp.bfloat16), latent, preferred_element_type=jnp.float32)
        stats = jnp.where(lanes((256, 128)) < 64, top, total)
        num[k, :, :, 0:512] = part.reshape(2, 128, 512)
        num[k, :, :, 512:640] = stats.reshape(2, 128, 128)
        ce(k).start()

    def core_merged(k):
        ce(k).wait_recv()
        return merge([(a[:, :512], a[:, 512:513], a[:, 576:577]) for a in (num[k, c], core_in[k])])

    def token(a, t):
        return a.reshape(4, QTOK, 16, a.shape[1])[:, t].reshape(64, a.shape[1])

    def half_rows(merged, t):
        rows, top, total = [token(a, t) for a in merged]
        return rows.astype(jnp.bfloat16), to_row(top) + to_row(total, 64)

    def half_parts(rows, stats):
        return rows.astype(jnp.float32), to_column(stats, 64), to_column(stats, 64, 64)

    def route_y(k):
        merged = core_merged(k)
        for t in range(QTOK):
            unit = 2 * k + t
            y_out[unit], y_ost[unit] = half_rows(merged, t)

            @pl.when(unit != y)
            def _():
                ys((unit - y + NY) % NY).start()

    def route_x(k):
        rows, top, total = core_merged(k)
        x_out[k - 2] = rows.astype(jnp.bfloat16)
        x_ost[k - 2, 0] = to_row(top)
        x_ost[k - 2, 1] = to_row(total)
        xs(k).start()

    def step(k, carry):
        send_core(k + 1)
        compute(k)

        @pl.when((k >= 1) & (k < 3))
        def _():
            route_y(k - 1)

        @pl.when(k >= 3)
        def _():
            route_x(k - 1)

        return carry

    send_core(1)
    cr().wait_recv()
    compute(0)
    lax.fori_loop(1, 7, step, 0)

    parts = [half_parts(y_out[y], y_ost[y])]
    for d in (1, 2, 3):
        ys(d).wait_recv()
        parts.append(half_parts(y_in[d - 1], y_ist[d - 1]))
    rows, top, total = merge(parts)
    v_out[...] = rows.astype(jnp.bfloat16)
    v_ost[...] = to_row(top) + to_row(total, 64)
    vs().start()

    compute(7)

    def own_pair(k, j):
        parts = [core_merged(k)]
        for side in range(2):
            xr(side, j).wait_recv()
            rows = x_in[side, j].astype(jnp.float32)
            parts.append((rows, to_column(x_ist[side, j, 0], 128), to_column(x_ist[side, j, 1], 128)))
        return merge(parts)

    merged = own_pair(6, 1 - my_j)
    for t in range(QTOK):
        w_out[t], w_ost[t] = half_rows(merged, t)
        ws(t).start()

    def owner_rows(column, rows, top, total):
        rows = rows.reshape(8, 8, 512)
        z_out[column] = jnp.concatenate([rows[:, :, :256], rows[:, :, 256:]], axis=1).astype(jnp.bfloat16)
        lane, row = lanes((64, 128)), iota((64, 128), 0) % 8
        stats = jnp.where(lane == row, top, jnp.where(lane == row + 8, total, 0.0))
        z_ost[column] = jnp.sum(stats.reshape(8, 8, 128), axis=1, keepdims=True)

    merged = own_pair(7, my_j)
    even = y % 2 == 0
    tokens = [[token(a, t) for a in merged] for t in range(QTOK)]
    owner_rows(1, *[jnp.where(even, b, a) for a, b in zip(*tokens)])
    for d in (4, 3, 5, 2, 6, 1, 7, 0):
        zs(1, d).start()
    parts = [tuple(jnp.where(even, a, b) for a, b in zip(*tokens))]
    vs().wait_recv()
    parts.append(half_parts(v_in[...], v_ist[...]))
    for s in range(2):
        wr(s).wait_recv()
        parts.append(half_parts(w_in[s], w_ist[s]))
    owner_rows(0, *merge(parts))
    for d in z_order:
        zs(0, d).start()
    z_in[0, z] = z_out[0, z]
    z_ist[0, z] = z_ost[0, z]

    for d in range(1, NZ):
        rz(d).wait_send()
    for d in (1, 2, 3):
        rx(d).wait_send()
        ys(d).wait_send()
    cr().wait_send()
    vs().wait_send()
    for t in range(QTOK):
        ws(t).wait_send()

    def drain(p, carry):
        for j in range(2):
            for d in range(1, NZ):
                zq(p, j, d).wait_send()
            for d in (1, 2, 3):
                pq(p, j, d).wait_send()
            cq(p, j).wait_send()
            ce(p * 2 + j).wait_send()
        xs(p + 2).wait_send()
        return carry

    lax.fori_loop(0, 4, drain, 0)

    for d in range(1, NZ):
        zr(0, d).wait_recv()
    for d in range(NZ):
        zr(1, d).wait_recv()

    got = z_in[...].reshape(16, 16, 256).astype(jnp.float32)
    stats = jnp.broadcast_to(z_ist[...].reshape(16, 1, 128), (16, 8, 128))
    lane, row = lanes((16, 8, 128)), iota((16, 8, 128), 1)
    tops = jnp.sum(jnp.where(lane == row, stats, 0.0), axis=2, keepdims=True)
    totals = jnp.sum(jnp.where(lane == row + 8, stats, 0.0), axis=2, keepdims=True)
    factor = jnp.exp2(tops - jnp.max(tops, axis=0, keepdims=True))
    total = jnp.sum(totals * factor, axis=0)
    left = jnp.sum(got[:, :8] * factor, axis=0)
    right = jnp.sum(got[:, 8:] * factor, axis=0)
    out[...] = (jnp.concatenate([left, right], axis=1) / total).astype(jnp.bfloat16)

    for d in range(1, NZ):
        zs(0, d).wait_send()
    for d in range(NZ):
        zs(1, d).wait_send()


def body(latent_cache, rope_cache, q_latent, q_rope, lengths):
    _, positions, width = latent_cache.shape
    q_pairs = q_latent.reshape(4, 2, *q_latent.shape[1:])
    anywhere = pl.BlockSpec(memory_space=pl.ANY)
    dma = pltpu.SemaphoreType.DMA
    vmem, bf16, f32 = pltpu.VMEM, jnp.bfloat16, jnp.float32
    return pl.pallas_call(
        kernel,
        out_shape=jax.ShapeDtypeStruct((8, width), jnp.bfloat16),
        in_specs=[anywhere] * 4 + [pl.BlockSpec(memory_space=pltpu.SMEM)],
        out_specs=pl.BlockSpec(memory_space=pltpu.VMEM),
        scratch_shapes=[
            vmem((8, positions, width), bf16),
            vmem((8, 128, positions), bf16),
            vmem((4, 2, NZ, QTOK, 16, width), bf16),
            vmem((QTOK, 1024), bf16),
            vmem((2, 4, NZ, 16, 128), bf16),
            vmem((8, 2, 128, 640), f32),
            vmem((8, 128, 640), f32),
            vmem((4, 128, width), bf16), vmem((4, 2, 1, 128), f32),
            vmem((2, 2, 128, width), bf16), vmem((2, 2, 2, 1, 128), f32),
            vmem((4, 64, width), bf16), vmem((4, 1, 128), f32),
            vmem((3, 64, width), bf16), vmem((3, 1, 128), f32),
            vmem((64, width), bf16), vmem((1, 128), f32),
            vmem((64, width), bf16), vmem((1, 128), f32),
            vmem((2, 64, width), bf16), vmem((2, 1, 128), f32),
            vmem((2, 64, width), bf16), vmem((2, 1, 128), f32),
            vmem((2, 8, 16, 256), bf16), vmem((2, 8, 1, 128), f32),
            vmem((2, 8, 16, 256), bf16), vmem((2, 8, 1, 128), f32),
            dma((8, 3)), dma((3,)),
            dma((4, 2, 7)), dma((4, 2, 7)), dma((7,)), dma((7,)),
            dma((4, 2, 3)), dma((4, 2, 3)), dma((3,)), dma((3,)),
            dma((4, 2)), dma((4, 2)), dma, dma,
            dma((8,)), dma((8,)),
            dma((2, 4)), dma((2, 2, 2)), dma((2, 3)), dma((2, 3)), dma((2,)), dma((2,)),
            dma((2, 2)), dma((2, 2)), dma((2, 2, 8)), dma((2, 2, 8)),
        ],
        compiler_params=pltpu.CompilerParams(
            collective_id=0, has_side_effects=True, vmem_limit_bytes=56 * 2**20
        ),
        cost_estimate=pl.CostEstimate(flops=5 * 10**9, bytes_accessed=10 * 10**6, transcendentals=2 * 10**6),
    )(latent_cache, rope_cache, q_pairs, q_rope, lengths)


def solution(mesh):
    in_specs = (
        P(None, ("ctx", "sub"), None),
        P(None, None, ("ctx", "sub")),
        P(None, None, "sub", None),
        P(None, None, "sub"),
        P(),
    )
    out_specs = P(("ctx", "sub"), None)
    return jax.shard_map(body, mesh=mesh, in_specs=in_specs, out_specs=out_specs, check_vma=False)
```

```python
import functools

import jax
import jax.numpy as jnp
from jax import lax
from jax.experimental import pallas as pl
from jax.experimental.pallas import tpu as pltpu
from jax.sharding import PartitionSpec as P

MESH = pl.DeviceIdType.MESH
NOPE = 128
QTOK = 2
NX, NY, NC, NZ = 4, 4, 2, 8
LOG2E = 1.4426950408889634
FLOOR = -16384.0


def place():
    ctx = lax.axis_index("ctx")
    return ctx // (NY * NC), (ctx // NC) % NY, ctx % NC, lax.axis_index("sub")


def device(x, y, c, z):
    return ((x * NY + y) * NC + c, z)


def iota(shape, axis):
    return lax.broadcasted_iota(jnp.int32, shape, axis)


def lanes(shape):
    return iota(shape, len(shape) - 1)


def to_row(column, offset=0):
    shape = (column.shape[0], 128)
    return jnp.sum(jnp.where(lanes(shape) == iota(shape, 0) + offset, column, 0.0), axis=0, keepdims=True)


def to_column(row, rows, offset=0):
    shape = (rows, 128)
    return jnp.sum(jnp.where(lanes(shape) == iota(shape, 0) + offset, row, 0.0), axis=1, keepdims=True)


def merge(parts):
    top = functools.reduce(jnp.maximum, [p[1] for p in parts])
    factors = [jnp.exp2(p[1] - top) for p in parts]
    num = functools.reduce(jnp.add, [p[0] * f for p, f in zip(parts, factors)])
    total = functools.reduce(jnp.add, [p[2] * f for p, f in zip(parts, factors)])
    return num, top, total


class Pair:
    def __init__(self, *copies):
        self.copies = copies

    def start(self):
        for copy in self.copies:
            copy.start()

    def wait_send(self):
        for copy in self.copies:
            copy.wait_send()

    def wait_recv(self):
        for copy in self.copies:
            copy.wait_recv()


def kernel(
    lat_hbm, rope_hbm, q_hbm, qr_hbm, lengths, out,
    kv, rr, q, qr_in, qr, num, core_in,
    x_out, x_ost, x_in, x_ist, y_out, y_ost, y_in, y_ist, v_out, v_ost, v_in, v_ist,
    w_out, w_ost, w_in, w_ist, z_out, z_ost, z_in, z_ist,
    kv_sem, own_sem, zq_send, zq_recv, rz_send, rz_recv, pq_send, pq_recv, rx_send, rx_recv,
    cq_send, cq_recv, cr_send, cr_recv, ce_send, ce_recv,
    x_send, x_recv, y_send, y_recv, v_send, v_recv, w_send, w_recv, z_send, z_recv,
):
    x, y, c, z = place()
    positions = kv.shape[1]
    first = (((x * NY + y) * NC + c) * NZ + z) * positions
    scale = (NOPE + 64) ** -0.5 * LOG2E
    my_j = y // 2
    y_pair = my_j * 2 + (1 - y % 2)

    def wrap_x(d):
        return (x + d) % NX

    def wrap_y(d):
        return (y + d) % NY

    def wrap_z(d):
        return (z + d) % NZ

    def step_dx(k):
        return jnp.where(k < 2, 2, jnp.where(k >= 6, 0, jnp.where(k % 2 == 0, 1, 3)))

    def step_j(k):
        late = (k == 4) | (k == 5) | (k == 7)
        return jnp.where(k < 2, k, jnp.where(late, my_j, 1 - my_j))

    def step_pair(k):
        return wrap_x(step_dx(k))

    def load_kv(k):
        b = step_pair(k) * 2 + step_j(k)
        return (
            pltpu.make_async_copy(lat_hbm.at[b], kv.at[k], kv_sem.at[k, 0]),
            pltpu.make_async_copy(rope_hbm.at[b], rr.at[k, pl.ds(0, 64)], kv_sem.at[k, 1]),
            pltpu.make_async_copy(rope_hbm.at[b], rr.at[k, pl.ds(64, 64)], kv_sem.at[k, 2]),
        )

    def remote(src, dst, send, recv, target):
        return pltpu.make_async_remote_copy(
            src_ref=src, dst_ref=dst, send_sem=send, recv_sem=recv, device_id=target, device_id_type=MESH
        )

    def lane_tile(i):
        return pl.ds(pl.multiple_of(i * 128, 128), 128)

    tiles = (lane_tile(y), lane_tile(x))

    own_q = [
        pltpu.make_async_copy(q_hbm.at[:, j, c, :, tiles[j]], q.at[:, j, z, c, :, tiles[j]], own_sem.at[j])
        for j in range(2)
    ]
    own_r = pltpu.make_async_copy(qr_hbm.at[2 * x + c], qr_in, own_sem.at[2])

    def zq(p, j, d):
        return remote(
            q_hbm.at[p, j, c, :, tiles[j]], q.at[p, j, z, c, :, tiles[j]],
            zq_send.at[p, j, d - 1], zq_recv.at[p, j, d - 1], device(x, y, c, wrap_z(d)),
        )

    def rz(d):
        return remote(
            qr.at[c, x, z], qr.at[c, x, z], rz_send.at[d - 1], rz_recv.at[d - 1], device(x, y, c, wrap_z(d))
        )

    def pq(p, j, d):
        target = device(x, wrap_y(d), c, z) if j == 0 else device(wrap_x(d), y, c, z)
        return remote(
            q.at[p, j, :, c, :, tiles[j]], q.at[p, j, :, c, :, tiles[j]],
            pq_send.at[p, j, d - 1], pq_recv.at[p, j, d - 1], target,
        )

    def pq_wait(p, j, d):
        piece = q.at[p, j, :, c, :, pl.ds(0, 128)]
        return remote(
            piece, piece, pq_send.at[p, j, d - 1], pq_recv.at[p, j, d - 1], device(x, wrap_y(d), c, z)
        )

    def rx(d):
        return remote(qr.at[c, x], qr.at[c, x], rx_send.at[d - 1], rx_recv.at[d - 1], device(wrap_x(d), y, c, z))

    def cq(p, j):
        return remote(
            q.at[p, j, :, c], q.at[p, j, :, c], cq_send.at[p, j], cq_recv.at[p, j], device(x, y, 1 - c, z)
        )

    def cr():
        return remote(qr.at[c], qr.at[c], cr_send, cr_recv, device(x, y, 1 - c, z))

    def ce(k):
        return remote(num.at[k, 1 - c], core_in.at[k], ce_send.at[k], ce_recv.at[k], device(x, y, 1 - c, z))

    def xs(k):
        side = k % 2
        j = step_j(k)
        target = device(wrap_x(1 + 2 * side), y, c, z)
        return Pair(
            remote(x_out.at[k - 2], x_in.at[side, j], x_send.at[0, k - 2], x_recv.at[0, side, j], target),
            remote(x_ost.at[k - 2], x_ist.at[side, j], x_send.at[1, k - 2], x_recv.at[1, side, j], target),
        )

    def xr(side, j):
        target = device(wrap_x(1), y, c, z)
        return Pair(
            remote(x_out.at[0], x_in.at[side, j], x_send.at[0, 0], x_recv.at[0, side, j], target),
            remote(x_ost.at[0], x_ist.at[side, j], x_send.at[1, 0], x_recv.at[1, side, j], target),
        )

    def ys(d):
        target = device(x, wrap_y(d), c, z)
        unit = wrap_y(d)
        return Pair(
            remote(y_out.at[unit], y_in.at[d - 1], y_send.at[0, d - 1], y_recv.at[0, d - 1], target),
            remote(y_ost.at[unit], y_ist.at[d - 1], y_send.at[1, d - 1], y_recv.at[1, d - 1], target),
        )

    def vs():
        target = device(wrap_x(2), y, c, z)
        return Pair(
            remote(v_out, v_in, v_send.at[0], v_recv.at[0], target),
            remote(v_ost, v_ist, v_send.at[1], v_recv.at[1], target),
        )

    def ws(t):
        target = device(x, (1 - my_j) * 2 + t, c, z)
        slot = y % 2
        return Pair(
            remote(w_out.at[t], w_in.at[slot], w_send.at[0, t], w_recv.at[0, slot], target),
            remote(w_ost.at[t], w_ist.at[slot], w_send.at[1, t], w_recv.at[1, slot], target),
        )

    def wr(s):
        target = device(x, (1 - my_j) * 2 + s, c, z)
        return Pair(
            remote(w_out.at[s], w_in.at[s], w_send.at[0, s], w_recv.at[0, s], target),
            remote(w_ost.at[s], w_ist.at[s], w_send.at[1, s], w_recv.at[1, s], target),
        )

    def zs(column, d):
        target = device(x, y if column == 0 else y_pair, c, wrap_z(d))
        there = wrap_z(d)
        return Pair(
            remote(z_out.at[column, there], z_in.at[column, z], z_send.at[0, column, d], z_recv.at[0, column, d], target),
            remote(z_ost.at[column, there], z_ist.at[column, z], z_send.at[1, column, d], z_recv.at[1, column, d], target),
        )

    def zr(column, d):
        source = (z - d + NZ) % NZ
        target = device(x, y_pair, c, wrap_z(d))
        return Pair(
            remote(z_out.at[column, z], z_in.at[column, source], z_send.at[0, column, d], z_recv.at[0, column, d], target),
            remote(z_ost.at[column, z], z_ist.at[column, source], z_send.at[1, column, d], z_recv.at[1, column, d], target),
        )

    partners = [device(x, y, c, wrap_z(d)) for d in range(1, NZ)]
    partners += [device(wrap_x(d), y, c, z) for d in (1, 2, 3)]
    partners += [device(x, wrap_y(d), c, z) for d in (1, 2, 3)]
    partners += [device(x, y, 1 - c, z)]
    barrier = pltpu.get_barrier_semaphore()
    for partner in partners:
        pl.semaphore_signal(barrier, inc=1, device_id=partner, device_id_type=MESH)
    own_r.start()
    for copy in own_q:
        copy.start()

    def load(k, carry):
        for copy in load_kv(k):
            copy.start()
        return carry

    lax.fori_loop(0, 8, load, 0)
    own_r.wait()
    spread = (lanes((16, 1024)) // 64) == iota((16, 1024), 0)
    head = iota((16, 128), 0)
    own_rope = jnp.zeros((16, 128), jnp.float32)
    raw = qr_in[...].astype(jnp.float32)
    for t in range(QTOK):
        wide = jnp.where(spread, raw[t : t + 1], 0.0)
        narrow = functools.reduce(jnp.add, [wide[:, i * 128 : (i + 1) * 128] for i in range(8)])
        own_rope = own_rope + jnp.where(head % 2 == t, narrow, pltpu.roll(narrow, 64, 1))
    qr[c, x, z] = own_rope.astype(jnp.bfloat16)
    pl.semaphore_wait(barrier, len(partners))

    z_order = (4, 3, 5, 2, 6, 1, 7)
    pair_order = (2, 1, 3, 0)
    for d in z_order:
        rz(d).start()

    def send_z(p, j):
        for d in z_order:
            zq(p, j, d).start()

    def wait_z(p, j):
        for d in z_order:
            zq(p, j, d).wait_recv()

    send_z(wrap_x(2), 0)
    for dx in (1, 3, 0, 2):
        send_z(wrap_x(dx), 1)
    for dx in pair_order[1:]:
        send_z(wrap_x(dx), 0)
    for copy in own_q:
        copy.wait()

    for d in z_order:
        rz(d).wait_recv()
    for d in (2, 1, 3):
        rx(d).start()
    wait_z(wrap_x(2), 0)
    for d in (2, 1, 3):
        pq(wrap_x(2), 0, d).start()
    for dx, ready in (
        (1, ((1, 3),)),
        (3, ((3, 1),)),
        (0, ((0, 2), (0, 3), (3, 2))),
        (2, ((2, 1), (1, 2), (0, 1), (2, 3), (1, 1), (3, 3), (2, 2))),
    ):
        wait_z(wrap_x(dx), 1)
        for pair, d in ready:
            pq(wrap_x(pair), 1, d).start()
    for dx in pair_order[1:]:
        wait_z(wrap_x(dx), 0)
        for d in (2, 1, 3):
            pq(wrap_x(dx), 0, d).start()

    def send_core(k):
        p, j = step_pair(k), step_j(k)
        for d in (1, 2, 3):
            pq_wait(p, j, d).wait_recv()
        cq(p, j).start()

    send_core(0)
    for d in (1, 2, 3):
        rx(d).wait_recv()
    cr().start()

    def compute(k):
        p, j = step_pair(k), step_j(k)
        cq(p, j).wait_recv()
        for copy in load_kv(k):
            copy.wait()
        query = q[p, j].reshape(256, 512)
        rope_q = qr[j, p]
        half = lanes((NZ, 16, 128)) // 64
        zero = jnp.zeros_like(rope_q)
        rope_q = jnp.stack([jnp.where(half == t, rope_q, zero) for t in range(QTOK)], axis=1).reshape(256, 128)
        latent = kv[k]
        scores = lax.dot_general(query, latent, (((1,), (1,)), ((), ())), preferred_element_type=jnp.float32)
        scores = scores + jnp.dot(rope_q, rr[k], preferred_element_type=jnp.float32)
        position = first + lanes((1, positions))
        length = lengths[p * 2 + j]
        bias = jnp.concatenate(
            [jnp.where(position < length - (QTOK - 1 - t), 0.0, -1e30) for t in range(QTOK)], axis=0
        )
        scores = scores.reshape(NZ, QTOK, 16, positions) * scale + bias.reshape(1, QTOK, 1, positions)
        scores = scores.reshape(256, positions)
        top = jnp.maximum(jnp.max(scores, axis=1, keepdims=True), FLOOR)
        weights = jnp.exp2(scores - top)
        total = jnp.sum(weights, axis=1, keepdims=True)
        part = jnp.dot(weights.astype(jnp.bfloat16), latent, preferred_element_type=jnp.float32)
        stats = jnp.where(lanes((256, 128)) < 64, top, total)
        num[k, :, :, 0:512] = part.reshape(2, 128, 512)
        num[k, :, :, 512:640] = stats.reshape(2, 128, 128)
        ce(k).start()

    def core_merged(k):
        ce(k).wait_recv()
        return merge([(a[:, :512], a[:, 512:513], a[:, 576:577]) for a in (num[k, c], core_in[k])])

    def token(a, t):
        return a.reshape(4, QTOK, 16, a.shape[1])[:, t].reshape(64, a.shape[1])

    def half_rows(merged, t):
        rows, top, total = [token(a, t) for a in merged]
        return rows.astype(jnp.bfloat16), to_row(top) + to_row(total, 64)

    def half_parts(rows, stats):
        return rows.astype(jnp.float32), to_column(stats, 64), to_column(stats, 64, 64)

    def route_y(k):
        merged = core_merged(k)
        for t in range(QTOK):
            unit = 2 * k + t
            y_out[unit], y_ost[unit] = half_rows(merged, t)

            @pl.when(unit != y)
            def _():
                ys((unit - y + NY) % NY).start()

    def route_x(k):
        rows, top, total = core_merged(k)
        x_out[k - 2] = rows.astype(jnp.bfloat16)
        x_ost[k - 2, 0] = to_row(top)
        x_ost[k - 2, 1] = to_row(total)
        xs(k).start()

    def step(k, carry):
        send_core(k + 1)
        compute(k)

        @pl.when((k >= 1) & (k < 3))
        def _():
            route_y(k - 1)

        @pl.when(k >= 3)
        def _():
            route_x(k - 1)

        return carry

    send_core(1)
    cr().wait_recv()
    compute(0)
    lax.fori_loop(1, 7, step, 0)

    parts = [half_parts(y_out[y], y_ost[y])]
    for d in (1, 2, 3):
        ys(d).wait_recv()
        parts.append(half_parts(y_in[d - 1], y_ist[d - 1]))
    rows, top, total = merge(parts)
    v_out[...] = rows.astype(jnp.bfloat16)
    v_ost[...] = to_row(top) + to_row(total, 64)
    vs().start()

    compute(7)

    def own_pair(k, j):
        parts = [core_merged(k)]
        for side in range(2):
            xr(side, j).wait_recv()
            rows = x_in[side, j].astype(jnp.float32)
            parts.append((rows, to_column(x_ist[side, j, 0], 128), to_column(x_ist[side, j, 1], 128)))
        return merge(parts)

    merged = own_pair(6, 1 - my_j)
    for t in range(QTOK):
        w_out[t], w_ost[t] = half_rows(merged, t)
        ws(t).start()

    def owner_rows(column, rows, top, total):
        rows = rows.reshape(8, 8, 512)
        z_out[column] = jnp.concatenate([rows[:, :, :256], rows[:, :, 256:]], axis=1).astype(jnp.bfloat16)
        lane, row = lanes((64, 128)), iota((64, 128), 0) % 8
        stats = jnp.where(lane == row, top, jnp.where(lane == row + 8, total, 0.0))
        z_ost[column] = jnp.sum(stats.reshape(8, 8, 128), axis=1, keepdims=True)

    merged = own_pair(7, my_j)
    even = y % 2 == 0
    tokens = [[token(a, t) for a in merged] for t in range(QTOK)]
    owner_rows(1, *[jnp.where(even, b, a) for a, b in zip(*tokens)])
    for d in (4, 3, 5, 2, 6, 1, 7, 0):
        zs(1, d).start()
    parts = [tuple(jnp.where(even, a, b) for a, b in zip(*tokens))]
    vs().wait_recv()
    parts.append(half_parts(v_in[...], v_ist[...]))
    for s in range(2):
        wr(s).wait_recv()
        parts.append(half_parts(w_in[s], w_ist[s]))
    owner_rows(0, *merge(parts))
    for d in z_order:
        zs(0, d).start()
    z_in[0, z] = z_out[0, z]
    z_ist[0, z] = z_ost[0, z]

    for d in range(1, NZ):
        rz(d).wait_send()
    for d in (1, 2, 3):
        rx(d).wait_send()
        ys(d).wait_send()
    cr().wait_send()
    vs().wait_send()
    for t in range(QTOK):
        ws(t).wait_send()

    def drain(p, carry):
        for j in range(2):
            for d in range(1, NZ):
                zq(p, j, d).wait_send()
            for d in (1, 2, 3):
                pq(p, j, d).wait_send()
            cq(p, j).wait_send()
            ce(p * 2 + j).wait_send()
        xs(p + 2).wait_send()
        return carry

    lax.fori_loop(0, 4, drain, 0)

    for d in range(1, NZ):
        zr(0, d).wait_recv()
    for d in range(NZ):
        zr(1, d).wait_recv()

    got = z_in[...].reshape(16, 16, 256).astype(jnp.float32)
    stats = jnp.broadcast_to(z_ist[...].reshape(16, 1, 128), (16, 8, 128))
    lane, row = lanes((16, 8, 128)), iota((16, 8, 128), 1)
    tops = jnp.sum(jnp.where(lane == row, stats, 0.0), axis=2, keepdims=True)
    totals = jnp.sum(jnp.where(lane == row + 8, stats, 0.0), axis=2, keepdims=True)
    factor = jnp.exp2(tops - jnp.max(tops, axis=0, keepdims=True))
    total = jnp.sum(totals * factor, axis=0)
    left = jnp.sum(got[:, :8] * factor, axis=0)
    right = jnp.sum(got[:, 8:] * factor, axis=0)
    out[...] = (jnp.concatenate([left, right], axis=1) / total).astype(jnp.bfloat16)

    for d in range(1, NZ):
        zs(0, d).wait_send()
    for d in range(NZ):
        zs(1, d).wait_send()


def body(latent_cache, rope_cache, q_latent, q_rope, lengths):
    _, positions, width = latent_cache.shape
    q_pairs = q_latent.reshape(4, 2, *q_latent.shape[1:])
    anywhere = pl.BlockSpec(memory_space=pl.ANY)
    dma = pltpu.SemaphoreType.DMA
    vmem, bf16, f32 = pltpu.VMEM, jnp.bfloat16, jnp.float32
    return pl.pallas_call(
        kernel,
        out_shape=jax.ShapeDtypeStruct((8, width), jnp.bfloat16),
        in_specs=[anywhere] * 4 + [pl.BlockSpec(memory_space=pltpu.SMEM)],
        out_specs=pl.BlockSpec(memory_space=pltpu.VMEM),
        scratch_shapes=[
            vmem((8, positions, width), bf16),
            vmem((8, 128, positions), bf16),
            vmem((4, 2, NZ, QTOK, 16, width), bf16),
            vmem((QTOK, 1024), bf16),
            vmem((2, 4, NZ, 16, 128), bf16),
            vmem((8, 2, 128, 640), f32),
            vmem((8, 128, 640), f32),
            vmem((4, 128, width), bf16), vmem((4, 2, 1, 128), f32),
            vmem((2, 2, 128, width), bf16), vmem((2, 2, 2, 1, 128), f32),
            vmem((4, 64, width), bf16), vmem((4, 1, 128), f32),
            vmem((3, 64, width), bf16), vmem((3, 1, 128), f32),
            vmem((64, width), bf16), vmem((1, 128), f32),
            vmem((64, width), bf16), vmem((1, 128), f32),
            vmem((2, 64, width), bf16), vmem((2, 1, 128), f32),
            vmem((2, 64, width), bf16), vmem((2, 1, 128), f32),
            vmem((2, 8, 16, 256), bf16), vmem((2, 8, 1, 128), f32),
            vmem((2, 8, 16, 256), bf16), vmem((2, 8, 1, 128), f32),
            dma((8, 3)), dma((3,)),
            dma((4, 2, 7)), dma((4, 2, 7)), dma((7,)), dma((7,)),
            dma((4, 2, 3)), dma((4, 2, 3)), dma((3,)), dma((3,)),
            dma((4, 2)), dma((4, 2)), dma, dma,
            dma((8,)), dma((8,)),
            dma((2, 4)), dma((2, 2, 2)), dma((2, 3)), dma((2, 3)), dma((2,)), dma((2,)),
            dma((2, 2)), dma((2, 2)), dma((2, 2, 8)), dma((2, 2, 8)),
        ],
        compiler_params=pltpu.CompilerParams(
            collective_id=0, has_side_effects=True, vmem_limit_bytes=56 * 2**20
        ),
        cost_estimate=pl.CostEstimate(flops=5 * 10**9, bytes_accessed=10 * 10**6, transcendentals=2 * 10**6),
    )(latent_cache, rope_cache, q_pairs, q_rope, lengths)


def solution(mesh):
    in_specs = (
        P(None, ("ctx", "sub"), None),
        P(None, None, ("ctx", "sub")),
        P(None, None, "sub", None),
        P(None, None, "sub"),
        P(),
    )
    out_specs = P(("ctx", "sub"), None)
    return jax.shard_map(body, mesh=mesh, in_specs=in_specs, out_specs=out_specs, check_vma=False)
```

```python
import functools

import jax
import jax.numpy as jnp
from jax import lax
from jax.experimental import pallas as pl
from jax.experimental.pallas import tpu as pltpu
from jax.sharding import PartitionSpec as P

MESH = pl.DeviceIdType.MESH
NOPE = 128
QTOK = 2
NX, NY, NC, NZ = 4, 4, 2, 8
LOG2E = 1.4426950408889634
FLOOR = -16384.0


def place():
    ctx = lax.axis_index("ctx")
    return ctx // (NY * NC), (ctx // NC) % NY, ctx % NC, lax.axis_index("sub")


def device(x, y, c, z):
    return ((x * NY + y) * NC + c, z)


def iota(shape, axis):
    return lax.broadcasted_iota(jnp.int32, shape, axis)


def lanes(shape):
    return iota(shape, len(shape) - 1)


def to_row(column, offset=0):
    shape = (column.shape[0], 128)
    return jnp.sum(jnp.where(lanes(shape) == iota(shape, 0) + offset, column, 0.0), axis=0, keepdims=True)


def to_column(row, rows, offset=0):
    shape = (rows, 128)
    return jnp.sum(jnp.where(lanes(shape) == iota(shape, 0) + offset, row, 0.0), axis=1, keepdims=True)


def merge(parts):
    top = functools.reduce(jnp.maximum, [p[1] for p in parts])
    factors = [jnp.exp2(p[1] - top) for p in parts]
    num = functools.reduce(jnp.add, [p[0] * f for p, f in zip(parts, factors)])
    total = functools.reduce(jnp.add, [p[2] * f for p, f in zip(parts, factors)])
    return num, top, total


class Pair:
    def __init__(self, *copies):
        self.copies = copies

    def start(self):
        for copy in self.copies:
            copy.start()

    def wait_send(self):
        for copy in self.copies:
            copy.wait_send()

    def wait_recv(self):
        for copy in self.copies:
            copy.wait_recv()


def kernel(
    lat_hbm, rope_hbm, q_hbm, qr_hbm, lengths, out,
    kv, rr, q, qr_in, qr, num, core_in,
    x_out, x_ost, x_in, x_ist, y_out, y_ost, y_in, y_ist, v_out, v_ost, v_in, v_ist,
    w_out, w_ost, w_in, w_ist, z_out, z_ost, z_in, z_ist,
    kv_sem, own_sem, zq_send, zq_recv, rz_send, rz_recv, pq_send, pq_recv, rx_send, rx_recv,
    cq_send, cq_recv, cr_send, cr_recv, ce_send, ce_recv,
    x_send, x_recv, y_send, y_recv, v_send, v_recv, w_send, w_recv, z_send, z_recv,
):
    x, y, c, z = place()
    positions = kv.shape[1]
    first = (((x * NY + y) * NC + c) * NZ + z) * positions
    scale = (NOPE + 64) ** -0.5 * LOG2E
    my_j = y // 2
    y_pair = my_j * 2 + (1 - y % 2)

    def wrap_x(d):
        return (x + d) % NX

    def wrap_y(d):
        return (y + d) % NY

    def wrap_z(d):
        return (z + d) % NZ

    def step_dx(k):
        return jnp.where(k < 2, 2, jnp.where(k >= 6, 0, jnp.where(k % 2 == 0, 1, 3)))

    def step_j(k):
        late = (k == 4) | (k == 5) | (k == 7)
        return jnp.where(k < 2, k, jnp.where(late, my_j, 1 - my_j))

    def step_pair(k):
        return wrap_x(step_dx(k))

    def load_kv(k):
        b = step_pair(k) * 2 + step_j(k)
        return (
            pltpu.make_async_copy(lat_hbm.at[b], kv.at[k], kv_sem.at[k, 0]),
            pltpu.make_async_copy(rope_hbm.at[b], rr.at[k, pl.ds(0, 64)], kv_sem.at[k, 1]),
            pltpu.make_async_copy(rope_hbm.at[b], rr.at[k, pl.ds(64, 64)], kv_sem.at[k, 2]),
        )

    def remote(src, dst, send, recv, target):
        return pltpu.make_async_remote_copy(
            src_ref=src, dst_ref=dst, send_sem=send, recv_sem=recv, device_id=target, device_id_type=MESH
        )

    def lane_tile(i):
        return pl.ds(pl.multiple_of(i * 128, 128), 128)

    tiles = (lane_tile(y), lane_tile(x))

    own_q = [
        pltpu.make_async_copy(q_hbm.at[:, j, c, :, tiles[j]], q.at[:, j, z, c, :, tiles[j]], own_sem.at[j])
        for j in range(2)
    ]
    own_r = pltpu.make_async_copy(qr_hbm.at[2 * x + c], qr_in, own_sem.at[2])

    def zq(p, j, d):
        return remote(
            q_hbm.at[p, j, c, :, tiles[j]], q.at[p, j, z, c, :, tiles[j]],
            zq_send.at[p, j, d - 1], zq_recv.at[p, j, d - 1], device(x, y, c, wrap_z(d)),
        )

    def rz(d):
        return remote(
            qr.at[c, x, z], qr.at[c, x, z], rz_send.at[d - 1], rz_recv.at[d - 1], device(x, y, c, wrap_z(d))
        )

    def pq(p, j, d):
        target = device(x, wrap_y(d), c, z) if j == 0 else device(wrap_x(d), y, c, z)
        return remote(
            q.at[p, j, :, c, :, tiles[j]], q.at[p, j, :, c, :, tiles[j]],
            pq_send.at[p, j, d - 1], pq_recv.at[p, j, d - 1], target,
        )

    def pq_wait(p, j, d):
        piece = q.at[p, j, :, c, :, pl.ds(0, 128)]
        return remote(
            piece, piece, pq_send.at[p, j, d - 1], pq_recv.at[p, j, d - 1], device(x, wrap_y(d), c, z)
        )

    def rx(d):
        return remote(qr.at[c, x], qr.at[c, x], rx_send.at[d - 1], rx_recv.at[d - 1], device(wrap_x(d), y, c, z))

    def cq(p, j):
        return remote(
            q.at[p, j, :, c], q.at[p, j, :, c], cq_send.at[p, j], cq_recv.at[p, j], device(x, y, 1 - c, z)
        )

    def cr():
        return remote(qr.at[c], qr.at[c], cr_send, cr_recv, device(x, y, 1 - c, z))

    def ce(k):
        return remote(num.at[k, 1 - c], core_in.at[k], ce_send.at[k], ce_recv.at[k], device(x, y, 1 - c, z))

    def xs(k):
        side = k % 2
        j = step_j(k)
        target = device(wrap_x(1 + 2 * side), y, c, z)
        return Pair(
            remote(x_out.at[k - 2], x_in.at[side, j], x_send.at[0, k - 2], x_recv.at[0, side, j], target),
            remote(x_ost.at[k - 2], x_ist.at[side, j], x_send.at[1, k - 2], x_recv.at[1, side, j], target),
        )

    def xr(side, j):
        target = device(wrap_x(1), y, c, z)
        return Pair(
            remote(x_out.at[0], x_in.at[side, j], x_send.at[0, 0], x_recv.at[0, side, j], target),
            remote(x_ost.at[0], x_ist.at[side, j], x_send.at[1, 0], x_recv.at[1, side, j], target),
        )

    def ys(d):
        target = device(x, wrap_y(d), c, z)
        unit = wrap_y(d)
        return Pair(
            remote(y_out.at[unit], y_in.at[d - 1], y_send.at[0, d - 1], y_recv.at[0, d - 1], target),
            remote(y_ost.at[unit], y_ist.at[d - 1], y_send.at[1, d - 1], y_recv.at[1, d - 1], target),
        )

    def vs():
        target = device(wrap_x(2), y, c, z)
        return Pair(
            remote(v_out, v_in, v_send.at[0], v_recv.at[0], target),
            remote(v_ost, v_ist, v_send.at[1], v_recv.at[1], target),
        )

    def ws(t):
        target = device(x, (1 - my_j) * 2 + t, c, z)
        slot = y % 2
        return Pair(
            remote(w_out.at[t], w_in.at[slot], w_send.at[0, t], w_recv.at[0, slot], target),
            remote(w_ost.at[t], w_ist.at[slot], w_send.at[1, t], w_recv.at[1, slot], target),
        )

    def wr(s):
        target = device(x, (1 - my_j) * 2 + s, c, z)
        return Pair(
            remote(w_out.at[s], w_in.at[s], w_send.at[0, s], w_recv.at[0, s], target),
            remote(w_ost.at[s], w_ist.at[s], w_send.at[1, s], w_recv.at[1, s], target),
        )

    def zs(column, d):
        target = device(x, y if column == 0 else y_pair, c, wrap_z(d))
        there = wrap_z(d)
        return Pair(
            remote(z_out.at[column, there], z_in.at[column, z], z_send.at[0, column, d], z_recv.at[0, column, d], target),
            remote(z_ost.at[column, there], z_ist.at[column, z], z_send.at[1, column, d], z_recv.at[1, column, d], target),
        )

    def zr(column, d):
        source = (z - d + NZ) % NZ
        target = device(x, y_pair, c, wrap_z(d))
        return Pair(
            remote(z_out.at[column, z], z_in.at[column, source], z_send.at[0, column, d], z_recv.at[0, column, d], target),
            remote(z_ost.at[column, z], z_ist.at[column, source], z_send.at[1, column, d], z_recv.at[1, column, d], target),
        )

    partners = [device(x, y, c, wrap_z(d)) for d in range(1, NZ)]
    partners += [device(wrap_x(d), y, c, z) for d in (1, 2, 3)]
    partners += [device(x, wrap_y(d), c, z) for d in (1, 2, 3)]
    partners += [device(x, y, 1 - c, z)]
    barrier = pltpu.get_barrier_semaphore()
    for partner in partners:
        pl.semaphore_signal(barrier, inc=1, device_id=partner, device_id_type=MESH)
    own_r.start()
    for copy in own_q:
        copy.start()

    def load(k, carry):
        for copy in load_kv(k):
            copy.start()
        return carry

    lax.fori_loop(0, 8, load, 0)
    own_r.wait()
    spread = (lanes((16, 1024)) // 64) == iota((16, 1024), 0)
    head = iota((16, 128), 0)
    own_rope = jnp.zeros((16, 128), jnp.float32)
    raw = qr_in[...].astype(jnp.float32)
    for t in range(QTOK):
        wide = jnp.where(spread, raw[t : t + 1], 0.0)
        narrow = functools.reduce(jnp.add, [wide[:, i * 128 : (i + 1) * 128] for i in range(8)])
        own_rope = own_rope + jnp.where(head % 2 == t, narrow, pltpu.roll(narrow, 64, 1))
    qr[c, x, z] = own_rope.astype(jnp.bfloat16)
    pl.semaphore_wait(barrier, len(partners))

    z_order = (4, 3, 5, 2, 6, 1, 7)
    pair_order = (2, 1, 3, 0)
    for d in z_order:
        rz(d).start()

    def send_z(p, j):
        for d in z_order:
            zq(p, j, d).start()

    def wait_z(p, j):
        for d in z_order:
            zq(p, j, d).wait_recv()

    send_z(wrap_x(2), 0)
    for dx in (1, 3, 0, 2):
        send_z(wrap_x(dx), 1)
    for dx in pair_order[1:]:
        send_z(wrap_x(dx), 0)
    for copy in own_q:
        copy.wait()

    for d in z_order:
        rz(d).wait_recv()
    for d in (2, 1, 3):
        rx(d).start()
    wait_z(wrap_x(2), 0)
    for d in (2, 1, 3):
        pq(wrap_x(2), 0, d).start()
    for dx, ready in (
        (1, ((1, 3),)),
        (3, ((3, 1),)),
        (0, ((0, 2), (0, 3), (3, 2))),
        (2, ((2, 1), (1, 2), (0, 1), (2, 3), (1, 1), (3, 3), (2, 2))),
    ):
        wait_z(wrap_x(dx), 1)
        for pair, d in ready:
            pq(wrap_x(pair), 1, d).start()
    for dx in pair_order[1:]:
        wait_z(wrap_x(dx), 0)
        for d in (2, 1, 3):
            pq(wrap_x(dx), 0, d).start()

    def send_core(k):
        p, j = step_pair(k), step_j(k)
        for d in (1, 2, 3):
            pq_wait(p, j, d).wait_recv()
        cq(p, j).start()

    send_core(0)
    for d in (1, 2, 3):
        rx(d).wait_recv()
    cr().start()

    def compute(k):
        p, j = step_pair(k), step_j(k)
        cq(p, j).wait_recv()
        for copy in load_kv(k):
            copy.wait()
        query = q[p, j].reshape(256, 512)
        rope_q = qr[j, p]
        half = lanes((NZ, 16, 128)) // 64
        zero = jnp.zeros_like(rope_q)
        rope_q = jnp.stack([jnp.where(half == t, rope_q, zero) for t in range(QTOK)], axis=1).reshape(256, 128)
        latent = kv[k]
        scores = lax.dot_general(query, latent, (((1,), (1,)), ((), ())), preferred_element_type=jnp.float32)
        scores = scores + jnp.dot(rope_q, rr[k], preferred_element_type=jnp.float32)
        position = first + lanes((1, positions))
        length = lengths[p * 2 + j]
        bias = jnp.concatenate(
            [jnp.where(position < length - (QTOK - 1 - t), 0.0, -1e30) for t in range(QTOK)], axis=0
        )
        scores = scores.reshape(NZ, QTOK, 16, positions) * scale + bias.reshape(1, QTOK, 1, positions)
        scores = scores.reshape(256, positions)
        top = jnp.maximum(jnp.max(scores, axis=1, keepdims=True), FLOOR)
        weights = jnp.exp2(scores - top)
        total = jnp.sum(weights, axis=1, keepdims=True)
        part = jnp.dot(weights.astype(jnp.bfloat16), latent, preferred_element_type=jnp.float32)
        stats = jnp.where(lanes((256, 128)) < 64, top, total)
        num[k, :, :, 0:512] = part.reshape(2, 128, 512)
        num[k, :, :, 512:640] = stats.reshape(2, 128, 128)
        ce(k).start()

    def core_merged(k):
        ce(k).wait_recv()
        return merge([(a[:, :512], a[:, 512:513], a[:, 576:577]) for a in (num[k, c], core_in[k])])

    def token(a, t):
        return a.reshape(4, QTOK, 16, a.shape[1])[:, t].reshape(64, a.shape[1])

    def half_rows(merged, t):
        rows, top, total = [token(a, t) for a in merged]
        return rows.astype(jnp.bfloat16), to_row(top) + to_row(total, 64)

    def half_parts(rows, stats):
        return rows.astype(jnp.float32), to_column(stats, 64), to_column(stats, 64, 64)

    def route_y(k):
        merged = core_merged(k)
        for t in range(QTOK):
            unit = 2 * k + t
            y_out[unit], y_ost[unit] = half_rows(merged, t)

            @pl.when(unit != y)
            def _():
                ys((unit - y + NY) % NY).start()

    def route_x(k):
        rows, top, total = core_merged(k)
        x_out[k - 2] = rows.astype(jnp.bfloat16)
        x_ost[k - 2, 0] = to_row(top)
        x_ost[k - 2, 1] = to_row(total)
        xs(k).start()

    def step(k, carry):
        send_core(k + 1)
        compute(k)

        @pl.when((k >= 1) & (k < 3))
        def _():
            route_y(k - 1)

        @pl.when(k >= 3)
        def _():
            route_x(k - 1)

        return carry

    send_core(1)
    cr().wait_recv()
    compute(0)
    lax.fori_loop(1, 7, step, 0)

    compute(7)

    def own_pair(k, j):
        parts = [core_merged(k)]
        for side in range(2):
            xr(side, j).wait_recv()
            rows = x_in[side, j].astype(jnp.float32)
            parts.append((rows, to_column(x_ist[side, j, 0], 128), to_column(x_ist[side, j, 1], 128)))
        return merge(parts)

    merged = own_pair(6, 1 - my_j)
    for t in range(QTOK):
        w_out[t], w_ost[t] = half_rows(merged, t)
        ws(t).start()

    def owner_rows(column, rows, top, total):
        rows = rows.reshape(8, 8, 512)
        z_out[column] = jnp.concatenate([rows[:, :, :256], rows[:, :, 256:]], axis=1).astype(jnp.bfloat16)
        lane, row = lanes((64, 128)), iota((64, 128), 0) % 8
        stats = jnp.where(lane == row, top, jnp.where(lane == row + 8, total, 0.0))
        z_ost[column] = jnp.sum(stats.reshape(8, 8, 128), axis=1, keepdims=True)

    parts = [half_parts(y_out[y], y_ost[y])]
    for d in (1, 2, 3):
        ys(d).wait_recv()
        parts.append(half_parts(y_in[d - 1], y_ist[d - 1]))
    rows, top, total = merge(parts)
    v_out[...] = rows.astype(jnp.bfloat16)
    v_ost[...] = to_row(top) + to_row(total, 64)
    vs().start()

    merged = own_pair(7, my_j)
    even = y % 2 == 0
    tokens = [[token(a, t) for a in merged] for t in range(QTOK)]
    owner_rows(1, *[jnp.where(even, b, a) for a, b in zip(*tokens)])
    for d in (4, 3, 5, 2, 6, 1, 7, 0):
        zs(1, d).start()
    parts = [tuple(jnp.where(even, a, b) for a, b in zip(*tokens))]
    vs().wait_recv()
    parts.append(half_parts(v_in[...], v_ist[...]))
    for s in range(2):
        wr(s).wait_recv()
        parts.append(half_parts(w_in[s], w_ist[s]))
    owner_rows(0, *merge(parts))
    for d in z_order:
        zs(0, d).start()
    z_in[0, z] = z_out[0, z]
    z_ist[0, z] = z_ost[0, z]

    for d in range(1, NZ):
        rz(d).wait_send()
    for d in (1, 2, 3):
        rx(d).wait_send()
        ys(d).wait_send()
    cr().wait_send()
    vs().wait_send()
    for t in range(QTOK):
        ws(t).wait_send()

    def drain(p, carry):
        for j in range(2):
            for d in range(1, NZ):
                zq(p, j, d).wait_send()
            for d in (1, 2, 3):
                pq(p, j, d).wait_send()
            cq(p, j).wait_send()
            ce(p * 2 + j).wait_send()
        xs(p + 2).wait_send()
        return carry

    lax.fori_loop(0, 4, drain, 0)

    for d in range(1, NZ):
        zr(0, d).wait_recv()
    for d in range(NZ):
        zr(1, d).wait_recv()

    got = z_in[...].reshape(16, 16, 256).astype(jnp.float32)
    stats = jnp.broadcast_to(z_ist[...].reshape(16, 1, 128), (16, 8, 128))
    lane, row = lanes((16, 8, 128)), iota((16, 8, 128), 1)
    tops = jnp.sum(jnp.where(lane == row, stats, 0.0), axis=2, keepdims=True)
    totals = jnp.sum(jnp.where(lane == row + 8, stats, 0.0), axis=2, keepdims=True)
    factor = jnp.exp2(tops - jnp.max(tops, axis=0, keepdims=True))
    total = jnp.sum(totals * factor, axis=0)
    left = jnp.sum(got[:, :8] * factor, axis=0)
    right = jnp.sum(got[:, 8:] * factor, axis=0)
    out[...] = (jnp.concatenate([left, right], axis=1) / total).astype(jnp.bfloat16)

    for d in range(1, NZ):
        zs(0, d).wait_send()
    for d in range(NZ):
        zs(1, d).wait_send()


def body(latent_cache, rope_cache, q_latent, q_rope, lengths):
    _, positions, width = latent_cache.shape
    q_pairs = q_latent.reshape(4, 2, *q_latent.shape[1:])
    anywhere = pl.BlockSpec(memory_space=pl.ANY)
    dma = pltpu.SemaphoreType.DMA
    vmem, bf16, f32 = pltpu.VMEM, jnp.bfloat16, jnp.float32
    return pl.pallas_call(
        kernel,
        out_shape=jax.ShapeDtypeStruct((8, width), jnp.bfloat16),
        in_specs=[anywhere] * 4 + [pl.BlockSpec(memory_space=pltpu.SMEM)],
        out_specs=pl.BlockSpec(memory_space=pltpu.VMEM),
        scratch_shapes=[
            vmem((8, positions, width), bf16),
            vmem((8, 128, positions), bf16),
            vmem((4, 2, NZ, QTOK, 16, width), bf16),
            vmem((QTOK, 1024), bf16),
            vmem((2, 4, NZ, 16, 128), bf16),
            vmem((8, 2, 128, 640), f32),
            vmem((8, 128, 640), f32),
            vmem((4, 128, width), bf16), vmem((4, 2, 1, 128), f32),
            vmem((2, 2, 128, width), bf16), vmem((2, 2, 2, 1, 128), f32),
            vmem((4, 64, width), bf16), vmem((4, 1, 128), f32),
            vmem((3, 64, width), bf16), vmem((3, 1, 128), f32),
            vmem((64, width), bf16), vmem((1, 128), f32),
            vmem((64, width), bf16), vmem((1, 128), f32),
            vmem((2, 64, width), bf16), vmem((2, 1, 128), f32),
            vmem((2, 64, width), bf16), vmem((2, 1, 128), f32),
            vmem((2, 8, 16, 256), bf16), vmem((2, 8, 1, 128), f32),
            vmem((2, 8, 16, 256), bf16), vmem((2, 8, 1, 128), f32),
            dma((8, 3)), dma((3,)),
            dma((4, 2, 7)), dma((4, 2, 7)), dma((7,)), dma((7,)),
            dma((4, 2, 3)), dma((4, 2, 3)), dma((3,)), dma((3,)),
            dma((4, 2)), dma((4, 2)), dma, dma,
            dma((8,)), dma((8,)),
            dma((2, 4)), dma((2, 2, 2)), dma((2, 3)), dma((2, 3)), dma((2,)), dma((2,)),
            dma((2, 2)), dma((2, 2)), dma((2, 2, 8)), dma((2, 2, 8)),
        ],
        compiler_params=pltpu.CompilerParams(
            collective_id=0, has_side_effects=True, vmem_limit_bytes=56 * 2**20
        ),
        cost_estimate=pl.CostEstimate(flops=5 * 10**9, bytes_accessed=10 * 10**6, transcendentals=2 * 10**6),
    )(latent_cache, rope_cache, q_pairs, q_rope, lengths)


def solution(mesh):
    in_specs = (
        P(None, ("ctx", "sub"), None),
        P(None, None, ("ctx", "sub")),
        P(None, None, "sub", None),
        P(None, None, "sub"),
        P(),
    )
    out_specs = P(("ctx", "sub"), None)
    return jax.shard_map(body, mesh=mesh, in_specs=in_specs, out_specs=out_specs, check_vma=False)
```

```python
import functools

import jax
import jax.numpy as jnp
from jax import lax
from jax.experimental import pallas as pl
from jax.experimental.pallas import tpu as pltpu
from jax.sharding import PartitionSpec as P

MESH = pl.DeviceIdType.MESH
NOPE = 128
QTOK = 2
NX, NY, NC, NZ = 4, 4, 2, 8
LOG2E = 1.4426950408889634
FLOOR = -16384.0


def place():
    ctx = lax.axis_index("ctx")
    return ctx // (NY * NC), (ctx // NC) % NY, ctx % NC, lax.axis_index("sub")


def device(x, y, c, z):
    return ((x * NY + y) * NC + c, z)


def iota(shape, axis):
    return lax.broadcasted_iota(jnp.int32, shape, axis)


def lanes(shape):
    return iota(shape, len(shape) - 1)


def to_row(column, offset=0):
    shape = (column.shape[0], 128)
    return jnp.sum(jnp.where(lanes(shape) == iota(shape, 0) + offset, column, 0.0), axis=0, keepdims=True)


def to_column(row, rows, offset=0):
    shape = (rows, 128)
    return jnp.sum(jnp.where(lanes(shape) == iota(shape, 0) + offset, row, 0.0), axis=1, keepdims=True)


def merge(parts):
    top = functools.reduce(jnp.maximum, [p[1] for p in parts])
    factors = [jnp.exp2(p[1] - top) for p in parts]
    num = functools.reduce(jnp.add, [p[0] * f for p, f in zip(parts, factors)])
    total = functools.reduce(jnp.add, [p[2] * f for p, f in zip(parts, factors)])
    return num, top, total


class Pair:
    def __init__(self, *copies):
        self.copies = copies

    def start(self):
        for copy in self.copies:
            copy.start()

    def wait_send(self):
        for copy in self.copies:
            copy.wait_send()

    def wait_recv(self):
        for copy in self.copies:
            copy.wait_recv()


def kernel(
    lat_hbm, rope_hbm, q_hbm, qr_hbm, lengths, out,
    kv, rr, q, qr_in, qr, num, core_in,
    x_out, x_ost, x_in, x_ist, y_out, y_ost, y_in, y_ist, v_out, v_ost, v_in, v_ist,
    w_out, w_ost, w_in, w_ist, z_out, z_ost, z_in, z_ist,
    kv_sem, own_sem, zq_send, zq_recv, rz_send, rz_recv, pq_send, pq_recv, rx_send, rx_recv,
    cq_send, cq_recv, cr_send, cr_recv, ce_send, ce_recv,
    x_send, x_recv, y_send, y_recv, v_send, v_recv, w_send, w_recv, z_send, z_recv,
):
    x, y, c, z = place()
    positions = kv.shape[1]
    first = (((x * NY + y) * NC + c) * NZ + z) * positions
    scale = (NOPE + 64) ** -0.5 * LOG2E
    my_j = y // 2
    y_pair = my_j * 2 + (1 - y % 2)

    def wrap_x(d):
        return (x + d) % NX

    def wrap_y(d):
        return (y + d) % NY

    def wrap_z(d):
        return (z + d) % NZ

    def step_dx(k):
        return jnp.where(k < 2, 2, jnp.where(k >= 6, 0, jnp.where(k % 2 == 0, 1, 3)))

    def step_j(k):
        late = (k == 4) | (k == 5) | (k == 7)
        return jnp.where(k < 2, k, jnp.where(late, my_j, 1 - my_j))

    def step_pair(k):
        return wrap_x(step_dx(k))

    def load_kv(k):
        b = step_pair(k) * 2 + step_j(k)
        return (
            pltpu.make_async_copy(lat_hbm.at[b], kv.at[k], kv_sem.at[k, 0]),
            pltpu.make_async_copy(rope_hbm.at[b], rr.at[k, pl.ds(0, 64)], kv_sem.at[k, 1]),
            pltpu.make_async_copy(rope_hbm.at[b], rr.at[k, pl.ds(64, 64)], kv_sem.at[k, 2]),
        )

    def remote(src, dst, send, recv, target):
        return pltpu.make_async_remote_copy(
            src_ref=src, dst_ref=dst, send_sem=send, recv_sem=recv, device_id=target, device_id_type=MESH
        )

    def lane_tile(i):
        return pl.ds(pl.multiple_of(i * 128, 128), 128)

    tiles = (lane_tile(y), lane_tile(x))

    own_q = [
        pltpu.make_async_copy(q_hbm.at[:, j, c, :, tiles[j]], q.at[:, j, z, c, :, tiles[j]], own_sem.at[j])
        for j in range(2)
    ]
    own_r = pltpu.make_async_copy(qr_hbm.at[2 * x + c], qr_in, own_sem.at[2])

    def zq(p, j, d):
        return remote(
            q_hbm.at[p, j, c, :, tiles[j]], q.at[p, j, z, c, :, tiles[j]],
            zq_send.at[p, j, d - 1], zq_recv.at[p, j, d - 1], device(x, y, c, wrap_z(d)),
        )

    def rz(d):
        return remote(
            qr.at[c, x, z], qr.at[c, x, z], rz_send.at[d - 1], rz_recv.at[d - 1], device(x, y, c, wrap_z(d))
        )

    def pq(p, j, d):
        target = device(x, wrap_y(d), c, z) if j == 0 else device(wrap_x(d), y, c, z)
        return remote(
            q.at[p, j, :, c, :, tiles[j]], q.at[p, j, :, c, :, tiles[j]],
            pq_send.at[p, j, d - 1], pq_recv.at[p, j, d - 1], target,
        )

    def pq_wait(p, j, d):
        piece = q.at[p, j, :, c, :, pl.ds(0, 128)]
        return remote(
            piece, piece, pq_send.at[p, j, d - 1], pq_recv.at[p, j, d - 1], device(x, wrap_y(d), c, z)
        )

    def rx(d):
        return remote(qr.at[c, x], qr.at[c, x], rx_send.at[d - 1], rx_recv.at[d - 1], device(wrap_x(d), y, c, z))

    def cq(p, j):
        return remote(
            q.at[p, j, :, c], q.at[p, j, :, c], cq_send.at[p, j], cq_recv.at[p, j], device(x, y, 1 - c, z)
        )

    def cr():
        return remote(qr.at[c], qr.at[c], cr_send, cr_recv, device(x, y, 1 - c, z))

    def ce(k):
        return remote(num.at[k, 1 - c], core_in.at[k], ce_send.at[k], ce_recv.at[k], device(x, y, 1 - c, z))

    def xs(k):
        side = k % 2
        j = step_j(k)
        target = device(wrap_x(1 + 2 * side), y, c, z)
        return Pair(
            remote(x_out.at[k - 2], x_in.at[side, j], x_send.at[0, k - 2], x_recv.at[0, side, j], target),
            remote(x_ost.at[k - 2], x_ist.at[side, j], x_send.at[1, k - 2], x_recv.at[1, side, j], target),
        )

    def xr(side, j):
        target = device(wrap_x(1), y, c, z)
        return Pair(
            remote(x_out.at[0], x_in.at[side, j], x_send.at[0, 0], x_recv.at[0, side, j], target),
            remote(x_ost.at[0], x_ist.at[side, j], x_send.at[1, 0], x_recv.at[1, side, j], target),
        )

    def ys(d):
        target = device(x, wrap_y(d), c, z)
        unit = wrap_y(d)
        return Pair(
            remote(y_out.at[unit], y_in.at[d - 1], y_send.at[0, d - 1], y_recv.at[0, d - 1], target),
            remote(y_ost.at[unit], y_ist.at[d - 1], y_send.at[1, d - 1], y_recv.at[1, d - 1], target),
        )

    def vs():
        target = device(wrap_x(2), y, c, z)
        return Pair(
            remote(v_out, v_in, v_send.at[0], v_recv.at[0], target),
            remote(v_ost, v_ist, v_send.at[1], v_recv.at[1], target),
        )

    def ws(t):
        target = device(x, (1 - my_j) * 2 + t, c, z)
        slot = y % 2
        return Pair(
            remote(w_out.at[t], w_in.at[slot], w_send.at[0, t], w_recv.at[0, slot], target),
            remote(w_ost.at[t], w_ist.at[slot], w_send.at[1, t], w_recv.at[1, slot], target),
        )

    def wr(s):
        target = device(x, (1 - my_j) * 2 + s, c, z)
        return Pair(
            remote(w_out.at[s], w_in.at[s], w_send.at[0, s], w_recv.at[0, s], target),
            remote(w_ost.at[s], w_ist.at[s], w_send.at[1, s], w_recv.at[1, s], target),
        )

    def zs(column, d):
        target = device(x, y if column == 0 else y_pair, c, wrap_z(d))
        there = wrap_z(d)
        return Pair(
            remote(z_out.at[column, there], z_in.at[column, z], z_send.at[0, column, d], z_recv.at[0, column, d], target),
            remote(z_ost.at[column, there], z_ist.at[column, z], z_send.at[1, column, d], z_recv.at[1, column, d], target),
        )

    def zr(column, d):
        source = (z - d + NZ) % NZ
        target = device(x, y_pair, c, wrap_z(d))
        return Pair(
            remote(z_out.at[column, z], z_in.at[column, source], z_send.at[0, column, d], z_recv.at[0, column, d], target),
            remote(z_ost.at[column, z], z_ist.at[column, source], z_send.at[1, column, d], z_recv.at[1, column, d], target),
        )

    partners = [device(x, y, c, wrap_z(d)) for d in range(1, NZ)]
    partners += [device(wrap_x(d), y, c, z) for d in (1, 2, 3)]
    partners += [device(x, wrap_y(d), c, z) for d in (1, 2, 3)]
    partners += [device(x, y, 1 - c, z)]
    barrier = pltpu.get_barrier_semaphore()
    for partner in partners:
        pl.semaphore_signal(barrier, inc=1, device_id=partner, device_id_type=MESH)
    own_r.start()
    for copy in own_q:
        copy.start()

    def load(k, carry):
        for copy in load_kv(k):
            copy.start()
        return carry

    lax.fori_loop(0, 8, load, 0)
    own_r.wait()
    spread = (lanes((16, 1024)) // 64) == iota((16, 1024), 0)
    head = iota((16, 128), 0)
    own_rope = jnp.zeros((16, 128), jnp.float32)
    raw = qr_in[...].astype(jnp.float32)
    for t in range(QTOK):
        wide = jnp.where(spread, raw[t : t + 1], 0.0)
        narrow = functools.reduce(jnp.add, [wide[:, i * 128 : (i + 1) * 128] for i in range(8)])
        own_rope = own_rope + jnp.where(head % 2 == t, narrow, pltpu.roll(narrow, 64, 1))
    qr[c, x, z] = own_rope.astype(jnp.bfloat16)
    pl.semaphore_wait(barrier, len(partners))

    z_order = (4, 3, 5, 2, 6, 1, 7)
    pair_order = (2, 1, 3, 0)
    def send_z(p, j):
        for d in z_order:
            zq(p, j, d).start()

    def wait_z(p, j):
        for d in z_order:
            zq(p, j, d).wait_recv()

    send_z(wrap_x(2), 0)
    for d in z_order:
        rz(d).start()
    for dx in (1, 3, 0, 2):
        send_z(wrap_x(dx), 1)
    for dx in pair_order[1:]:
        send_z(wrap_x(dx), 0)
    for copy in own_q:
        copy.wait()

    wait_z(wrap_x(2), 0)
    for d in (2, 1, 3):
        pq(wrap_x(2), 0, d).start()
    for d in z_order:
        rz(d).wait_recv()
    for d in (2, 1, 3):
        rx(d).start()
    for dx, ready in (
        (1, ((1, 3),)),
        (3, ((3, 1),)),
        (0, ((0, 2), (0, 3), (3, 2))),
        (2, ((2, 1), (1, 2), (0, 1), (2, 3), (1, 1), (3, 3), (2, 2))),
    ):
        wait_z(wrap_x(dx), 1)
        for pair, d in ready:
            pq(wrap_x(pair), 1, d).start()
    for dx in pair_order[1:]:
        wait_z(wrap_x(dx), 0)
        for d in (2, 1, 3):
            pq(wrap_x(dx), 0, d).start()

    def send_core(k):
        p, j = step_pair(k), step_j(k)
        for d in (1, 2, 3):
            pq_wait(p, j, d).wait_recv()
        cq(p, j).start()

    send_core(0)
    for d in (1, 2, 3):
        rx(d).wait_recv()
    cr().start()

    def compute(k):
        p, j = step_pair(k), step_j(k)
        cq(p, j).wait_recv()
        for copy in load_kv(k):
            copy.wait()
        query = q[p, j].reshape(256, 512)
        rope_q = qr[j, p]
        half = lanes((NZ, 16, 128)) // 64
        zero = jnp.zeros_like(rope_q)
        rope_q = jnp.stack([jnp.where(half == t, rope_q, zero) for t in range(QTOK)], axis=1).reshape(256, 128)
        latent = kv[k]
        scores = lax.dot_general(query, latent, (((1,), (1,)), ((), ())), preferred_element_type=jnp.float32)
        scores = scores + jnp.dot(rope_q, rr[k], preferred_element_type=jnp.float32)
        position = first + lanes((1, positions))
        length = lengths[p * 2 + j]
        bias = jnp.concatenate(
            [jnp.where(position < length - (QTOK - 1 - t), 0.0, -1e30) for t in range(QTOK)], axis=0
        )
        scores = scores.reshape(NZ, QTOK, 16, positions) * scale + bias.reshape(1, QTOK, 1, positions)
        scores = scores.reshape(256, positions)
        top = jnp.maximum(jnp.max(scores, axis=1, keepdims=True), FLOOR)
        weights = jnp.exp2(scores - top)
        total = jnp.sum(weights, axis=1, keepdims=True)
        part = jnp.dot(weights.astype(jnp.bfloat16), latent, preferred_element_type=jnp.float32)
        stats = jnp.where(lanes((256, 128)) < 64, top, total)
        num[k, :, :, 0:512] = part.reshape(2, 128, 512)
        num[k, :, :, 512:640] = stats.reshape(2, 128, 128)
        ce(k).start()

    def core_merged(k):
        ce(k).wait_recv()
        return merge([(a[:, :512], a[:, 512:513], a[:, 576:577]) for a in (num[k, c], core_in[k])])

    def token(a, t):
        return a.reshape(4, QTOK, 16, a.shape[1])[:, t].reshape(64, a.shape[1])

    def half_rows(merged, t):
        rows, top, total = [token(a, t) for a in merged]
        return rows.astype(jnp.bfloat16), to_row(top) + to_row(total, 64)

    def half_parts(rows, stats):
        return rows.astype(jnp.float32), to_column(stats, 64), to_column(stats, 64, 64)

    def route_y(k):
        merged = core_merged(k)
        for t in range(QTOK):
            unit = 2 * k + t
            y_out[unit], y_ost[unit] = half_rows(merged, t)

            @pl.when(unit != y)
            def _():
                ys((unit - y + NY) % NY).start()

    def route_x(k):
        rows, top, total = core_merged(k)
        x_out[k - 2] = rows.astype(jnp.bfloat16)
        x_ost[k - 2, 0] = to_row(top)
        x_ost[k - 2, 1] = to_row(total)
        xs(k).start()

    def step(k, carry):
        send_core(k + 1)
        compute(k)

        @pl.when((k >= 1) & (k < 3))
        def _():
            route_y(k - 1)

        @pl.when(k >= 3)
        def _():
            route_x(k - 1)

        return carry

    send_core(1)
    cr().wait_recv()
    compute(0)
    lax.fori_loop(1, 7, step, 0)

    compute(7)

    def own_pair(k, j):
        parts = [core_merged(k)]
        for side in range(2):
            xr(side, j).wait_recv()
            rows = x_in[side, j].astype(jnp.float32)
            parts.append((rows, to_column(x_ist[side, j, 0], 128), to_column(x_ist[side, j, 1], 128)))
        return merge(parts)

    merged = own_pair(6, 1 - my_j)
    for t in range(QTOK):
        w_out[t], w_ost[t] = half_rows(merged, t)
        ws(t).start()

    def owner_rows(column, rows, top, total):
        rows = rows.reshape(8, 8, 512)
        z_out[column] = jnp.concatenate([rows[:, :, :256], rows[:, :, 256:]], axis=1).astype(jnp.bfloat16)
        lane, row = lanes((64, 128)), iota((64, 128), 0) % 8
        stats = jnp.where(lane == row, top, jnp.where(lane == row + 8, total, 0.0))
        z_ost[column] = jnp.sum(stats.reshape(8, 8, 128), axis=1, keepdims=True)

    parts = [half_parts(y_out[y], y_ost[y])]
    for d in (1, 2, 3):
        ys(d).wait_recv()
        parts.append(half_parts(y_in[d - 1], y_ist[d - 1]))
    rows, top, total = merge(parts)
    v_out[...] = rows.astype(jnp.bfloat16)
    v_ost[...] = to_row(top) + to_row(total, 64)
    vs().start()

    merged = own_pair(7, my_j)
    even = y % 2 == 0
    tokens = [[token(a, t) for a in merged] for t in range(QTOK)]
    owner_rows(1, *[jnp.where(even, b, a) for a, b in zip(*tokens)])
    for d in (4, 3, 5, 2, 6, 1, 7, 0):
        zs(1, d).start()
    parts = [tuple(jnp.where(even, a, b) for a, b in zip(*tokens))]
    vs().wait_recv()
    parts.append(half_parts(v_in[...], v_ist[...]))
    for s in range(2):
        wr(s).wait_recv()
        parts.append(half_parts(w_in[s], w_ist[s]))
    owner_rows(0, *merge(parts))
    for d in z_order:
        zs(0, d).start()
    z_in[0, z] = z_out[0, z]
    z_ist[0, z] = z_ost[0, z]

    for d in range(1, NZ):
        rz(d).wait_send()
    for d in (1, 2, 3):
        rx(d).wait_send()
        ys(d).wait_send()
    cr().wait_send()
    vs().wait_send()
    for t in range(QTOK):
        ws(t).wait_send()

    def drain(p, carry):
        for j in range(2):
            for d in range(1, NZ):
                zq(p, j, d).wait_send()
            for d in (1, 2, 3):
                pq(p, j, d).wait_send()
            cq(p, j).wait_send()
            ce(p * 2 + j).wait_send()
        xs(p + 2).wait_send()
        return carry

    lax.fori_loop(0, 4, drain, 0)

    for d in range(1, NZ):
        zr(0, d).wait_recv()
    for d in range(NZ):
        zr(1, d).wait_recv()

    got = z_in[...].reshape(16, 16, 256).astype(jnp.float32)
    stats = jnp.broadcast_to(z_ist[...].reshape(16, 1, 128), (16, 8, 128))
    lane, row = lanes((16, 8, 128)), iota((16, 8, 128), 1)
    tops = jnp.sum(jnp.where(lane == row, stats, 0.0), axis=2, keepdims=True)
    totals = jnp.sum(jnp.where(lane == row + 8, stats, 0.0), axis=2, keepdims=True)
    factor = jnp.exp2(tops - jnp.max(tops, axis=0, keepdims=True))
    total = jnp.sum(totals * factor, axis=0)
    left = jnp.sum(got[:, :8] * factor, axis=0)
    right = jnp.sum(got[:, 8:] * factor, axis=0)
    out[...] = (jnp.concatenate([left, right], axis=1) / total).astype(jnp.bfloat16)

    for d in range(1, NZ):
        zs(0, d).wait_send()
    for d in range(NZ):
        zs(1, d).wait_send()


def body(latent_cache, rope_cache, q_latent, q_rope, lengths):
    _, positions, width = latent_cache.shape
    q_pairs = q_latent.reshape(4, 2, *q_latent.shape[1:])
    anywhere = pl.BlockSpec(memory_space=pl.ANY)
    dma = pltpu.SemaphoreType.DMA
    vmem, bf16, f32 = pltpu.VMEM, jnp.bfloat16, jnp.float32
    return pl.pallas_call(
        kernel,
        out_shape=jax.ShapeDtypeStruct((8, width), jnp.bfloat16),
        in_specs=[anywhere] * 4 + [pl.BlockSpec(memory_space=pltpu.SMEM)],
        out_specs=pl.BlockSpec(memory_space=pltpu.VMEM),
        scratch_shapes=[
            vmem((8, positions, width), bf16),
            vmem((8, 128, positions), bf16),
            vmem((4, 2, NZ, QTOK, 16, width), bf16),
            vmem((QTOK, 1024), bf16),
            vmem((2, 4, NZ, 16, 128), bf16),
            vmem((8, 2, 128, 640), f32),
            vmem((8, 128, 640), f32),
            vmem((4, 128, width), bf16), vmem((4, 2, 1, 128), f32),
            vmem((2, 2, 128, width), bf16), vmem((2, 2, 2, 1, 128), f32),
            vmem((4, 64, width), bf16), vmem((4, 1, 128), f32),
            vmem((3, 64, width), bf16), vmem((3, 1, 128), f32),
            vmem((64, width), bf16), vmem((1, 128), f32),
            vmem((64, width), bf16), vmem((1, 128), f32),
            vmem((2, 64, width), bf16), vmem((2, 1, 128), f32),
            vmem((2, 64, width), bf16), vmem((2, 1, 128), f32),
            vmem((2, 8, 16, 256), bf16), vmem((2, 8, 1, 128), f32),
            vmem((2, 8, 16, 256), bf16), vmem((2, 8, 1, 128), f32),
            dma((8, 3)), dma((3,)),
            dma((4, 2, 7)), dma((4, 2, 7)), dma((7,)), dma((7,)),
            dma((4, 2, 3)), dma((4, 2, 3)), dma((3,)), dma((3,)),
            dma((4, 2)), dma((4, 2)), dma, dma,
            dma((8,)), dma((8,)),
            dma((2, 4)), dma((2, 2, 2)), dma((2, 3)), dma((2, 3)), dma((2,)), dma((2,)),
            dma((2, 2)), dma((2, 2)), dma((2, 2, 8)), dma((2, 2, 8)),
        ],
        compiler_params=pltpu.CompilerParams(
            collective_id=0, has_side_effects=True, vmem_limit_bytes=56 * 2**20
        ),
        cost_estimate=pl.CostEstimate(flops=5 * 10**9, bytes_accessed=10 * 10**6, transcendentals=2 * 10**6),
    )(latent_cache, rope_cache, q_pairs, q_rope, lengths)


def solution(mesh):
    in_specs = (
        P(None, ("ctx", "sub"), None),
        P(None, None, ("ctx", "sub")),
        P(None, None, "sub", None),
        P(None, None, "sub"),
        P(),
    )
    out_specs = P(("ctx", "sub"), None)
    return jax.shard_map(body, mesh=mesh, in_specs=in_specs, out_specs=out_specs, check_vma=False)
```
